128 devices in a mesh: dom: 2 (over core), cls: 64 (over z, y, x).
Axes of the slice: x: 4, y: 4, z: 4, core: 2. Of those that a mesh axis runs over, the one named last changes fastest.
Arguments:
- images: bfloat16 [12288, 4096], P(('cls', 'dom')), may hold values from -12 to 12, as said below
- precision: bfloat16 [12288], P(('cls', 'dom')), may hold values from 0.00048828125 to 0.048828125
- rotation_offset: int32 [12288], P(('cls', 'dom')), may hold values from 0 to 35
- classes: bfloat16 [200, 4096], P('dom'), may hold values from -4 to 4
- prior_blocks: int32 [128, 40], P('cls', 'dom'), may hold values from 0 to 1, as said below
Outputs:
- new_classes: float32 [200, 4096], P('dom')
- log_evidence: float32 [12288], P(('cls', 'dom'))
The draws below stay inside these ranges and needn't reach their ends.
Inputs may be any that keep to these rules, and one draw needn't show every extreme that they name: `images`: each image is a rotated class average scaled by a positive factor plus noise. `prior_blocks`: every particle block admits at least one class block.
All inputs are finite; a program needn't handle non-finite values.
Results may differ from the reference program's by a relative error of at most 0.0019.
Values may be sent and summed in bfloat16 or wider, within the bound.
No kernel may reach another device: no remote copies, remote signals or barrier semaphores. Data moves between devices by JAX's collectives and lax.ppermute only.
A program may use at most 64 MiB of HBM per device.

```python
import math
import jax
import jax.numpy as jnp
from jax import lax

FREQUENCIES = 64
IMAGE_REALS = 4096
ROTATIONS = 36
CLASSES = 200
CLASS_BLOCK = 5
PARTICLES_DEV = 96
PARTICLES = 12288
PART_BLOCKS = 128
CLASS_BLOCKS = 40
N_DOM = 2


def shared_bank(key):
    return jax.random.truncated_normal(key, -4.0, 4.0, (CLASSES, IMAGE_REALS), jnp.float32)


def turn_forward(bank_rows, turn_index):
    row_count = bank_rows.shape[0]
    angle_steps = turn_index[:, None] * jnp.arange(FREQUENCIES, dtype=jnp.int32)[None, :] % ROTATIONS
    angle = angle_steps.astype(jnp.float32) * (2.0 * math.pi / ROTATIONS)
    cosine = jnp.cos(angle)[:, :, None]
    sine_term = jnp.sin(angle)[:, :, None]
    split_parts = bank_rows.reshape(row_count, 2, FREQUENCIES, IMAGE_REALS // (2 * FREQUENCIES))
    real_part = split_parts[:, 0]
    imag_part = split_parts[:, 1]
    turned = jnp.stack([real_part * cosine + imag_part * sine_term, imag_part * cosine - real_part * sine_term], axis=1)
    return turned.reshape(row_count, IMAGE_REALS)


def draw_classes(key, part):
    class_bank = shared_bank(key)
    return class_bank.astype(jnp.bfloat16)


def draw_images(key, part):
    class_bank = shared_bank(key)
    key = jax.random.fold_in(key, 2)
    key_class, key_turn, key_scale, key_noise = jax.random.split(key, 4)
    source_class = jax.random.randint(key_class, (PARTICLES,), 0, CLASSES)
    turn_index = jax.random.randint(key_turn, (PARTICLES,), 0, ROTATIONS)
    amplitude = jax.random.uniform(key_scale, (PARTICLES, 1), jnp.float32, 0.1, 0.5)
    noise_field = jax.random.truncated_normal(key_noise, -4.0, 4.0, (PARTICLES, IMAGE_REALS), jnp.float32)
    signal = turn_forward(class_bank[source_class], turn_index)
    return (amplitude * signal + noise_field).astype(jnp.bfloat16)


def draw_prior_blocks(key, part):
    key = jax.random.fold_in(key, 3)
    key_density, key_values, key_forced = jax.random.split(key, 3)
    density = jax.random.randint(key_density, (PART_BLOCKS, 1), 1, 17)
    random_values = jax.random.randint(key_values, (PART_BLOCKS, CLASS_BLOCKS), 0, 16)
    forced = jax.random.randint(key_forced, (PART_BLOCKS, 1), 0, CLASS_BLOCKS)
    column_index = jnp.arange(CLASS_BLOCKS, dtype=jnp.int32)[None, :]
    allowed = jnp.logical_or(random_values < density, column_index == forced)
    return allowed.astype(jnp.int32)


def touch_ends(drawn, key, least, high):
    dims = drawn.shape
    spot = [jax.random.randint(jax.random.fold_in(key, axis), (), 0, dims[axis]) for axis in range(len(dims))]
    drawn = drawn.at[tuple(spot)].set(least)
    longest = dims.index(max(dims))
    spot[longest] = (spot[longest] + 1) % dims[longest]
    return drawn.at[tuple(spot)].set(high)


def block_levels(key, shape, cuts, smallest, largest):
    level = 1.0
    for dim, shards_of in cuts:
        heights = jax.random.uniform(jax.random.fold_in(jax.random.fold_in(key, 6), dim), (shards_of,), jnp.float32, smallest / len(cuts), largest / len(cuts))
        level = level * jnp.repeat(jnp.exp(heights), shape[dim] // shards_of).reshape((-1,) + (1,) * (len(shape) - 1 - dim))
    return level


def setup_inputs(seed: int = 0) -> dict:
    seeds = jax.random.split(jax.random.key(seed), 6)
    return {
        "images": draw_images(jax.random.fold_in(seeds[5], 71), 0),
        "precision": jnp.clip(jnp.exp(math.log(0.048828125) - 4.6051702 * jax.random.uniform(seeds[1], (PARTICLES,), jnp.float32) ** block_levels(seeds[1], (PARTICLES,), ((0, 128),), -0.2, 0.2)), 0.00048828125, 0.048828125).astype(jnp.bfloat16),
        "rotation_offset": touch_ends(jax.random.randint(seeds[2], (PARTICLES,), 0, ROTATIONS), jax.random.fold_in(seeds[2], 1), 0, ROTATIONS - 1).astype(jnp.int32),
        "classes": draw_classes(jax.random.fold_in(seeds[5], 71), 0),
        "prior_blocks": draw_prior_blocks(jax.random.fold_in(seeds[5], 71), 0),
    }


EXCLUDED = -1.0e30
PRIOR_WIDTH = 12.0
CLASS_PRIOR = 16.0


def trig_tables():
    angle_steps = (jnp.arange(ROTATIONS, dtype=jnp.int32)[:, None] * jnp.arange(FREQUENCIES, dtype=jnp.int32)[None, :]) % ROTATIONS
    angle = angle_steps.astype(jnp.float32) * (2.0 * math.pi / ROTATIONS)
    return jnp.cos(angle), jnp.sin(angle)


def rotate_bank(class_bank, cos_table, sin_table):
    bank_size, image_width = class_bank.shape
    split_parts = class_bank.astype(jnp.float32).reshape(bank_size, 1, 2, FREQUENCIES, image_width // (2 * FREQUENCIES))
    real_part = split_parts[:, :, 0]
    imag_part = split_parts[:, :, 1]
    cosine = cos_table[None, :, :, None]
    sine_term = sin_table[None, :, :, None]
    turned = jnp.stack([real_part * cosine + imag_part * sine_term, imag_part * cosine - real_part * sine_term], axis=2)
    return turned.reshape(bank_size * ROTATIONS, image_width).astype(jnp.bfloat16)


def back_rotate(aligned, cos_table, sin_table):
    bank_size = aligned.shape[0]
    image_width = aligned.shape[2]
    split_parts = aligned.reshape(bank_size, ROTATIONS, 2, FREQUENCIES, image_width // (2 * FREQUENCIES))
    real_part = split_parts[:, :, 0]
    imag_part = split_parts[:, :, 1]

    def turn_sum(values, trig_table):
        return jnp.einsum("brfg,rf->bfg", values, trig_table, precision=lax.Precision.HIGHEST)

    back_real = turn_sum(real_part, cos_table) - turn_sum(imag_part, sin_table)
    back_imag = turn_sum(imag_part, cos_table) + turn_sum(real_part, sin_table)
    return jnp.stack([back_real, back_imag], axis=1).reshape(bank_size, image_width)


def rotation_prior(offsets):
    offset_steps = (jnp.arange(ROTATIONS, dtype=jnp.int32)[None, :] - offsets[:, None]) % ROTATIONS
    distance = jnp.minimum(offset_steps, ROTATIONS - offset_steps).astype(jnp.float32)
    return -0.5 * (distance / PRIOR_WIDTH) * (distance / PRIOR_WIDTH)


def expand_mask(mask_rows, rows_each):
    widened = jnp.repeat(jnp.repeat(mask_rows, rows_each, axis=0), CLASS_BLOCK, axis=1)
    return widened == 1


def class_scores(particles, precision, offsets, class_bank, allowed, cos_table, sin_table):
    row_count = particles.shape[0]
    blocks = class_bank.shape[0] // CLASS_BLOCK
    turn_prior = rotation_prior(offsets)
    noise_precision = precision.astype(jnp.float32)

    def one_block(block_index):
        members = lax.dynamic_slice_in_dim(class_bank, block_index * CLASS_BLOCK, CLASS_BLOCK, 0)
        turned = rotate_bank(members, cos_table, sin_table)
        correlation = lax.dot_general(particles, turned, (((1,), (1,)), ((), ())), preferred_element_type=jnp.float32)
        correlation = correlation.reshape(row_count, CLASS_BLOCK, ROTATIONS)
        class_norms = jnp.sum(jnp.square(members.astype(jnp.float32)), axis=1)
        admitted = lax.dynamic_slice_in_dim(allowed, block_index * CLASS_BLOCK, CLASS_BLOCK, 1)
        score = noise_precision[:, None, None] * (correlation - 0.5 * class_norms[None, :, None]) + turn_prior[:, None, :]
        return jnp.where(admitted[:, :, None], score, EXCLUDED)

    return lax.map(one_block, jnp.arange(blocks, dtype=jnp.int32))


def class_sums(weights, particles, cos_table, sin_table):
    blocks = weights.shape[0]
    row_count = weights.shape[1]

    def one_block(block_weights):
        flat_weights = block_weights.reshape(row_count, CLASS_BLOCK * ROTATIONS)
        aligned = lax.dot_general(flat_weights, particles, (((0,), (0,)), ((), ())), preferred_element_type=jnp.float32)
        class_total = back_rotate(aligned.reshape(CLASS_BLOCK, ROTATIONS, -1), cos_table, sin_table)
        mass_total = jnp.sum(flat_weights.astype(jnp.float32), axis=0).reshape(CLASS_BLOCK, ROTATIONS).sum(axis=1)
        return class_total, mass_total

    class_total, mass_total = lax.map(one_block, weights)
    return class_total.reshape(blocks * CLASS_BLOCK, -1), mass_total.reshape(-1)


def reference(images, precision, rotation_offset, classes, prior_blocks):
    cos_table, sin_table = trig_tables()
    group_size = PARTICLES_DEV * N_DOM
    group_count = PARTICLES // group_size

    def one_group(running, inputs):
        class_total, mass_total = running
        particles, group_precision, offsets, mask_rows = inputs
        allowed = expand_mask(mask_rows, PARTICLES_DEV)
        scores = class_scores(particles, group_precision, offsets, classes, allowed, cos_table, sin_table)
        peak_score = jnp.max(scores, axis=(0, 2, 3))
        shifted = jnp.exp(scores - peak_score[None, :, None, None])
        total_mass = jnp.sum(shifted, axis=(0, 2, 3))
        weights = (shifted / total_mass[None, :, None, None]).astype(jnp.bfloat16)
        sums_here, masses_here = class_sums(weights, particles, cos_table, sin_table)
        return (class_total + sums_here, mass_total + masses_here), peak_score + jnp.log(total_mass)

    initial = (jnp.zeros((CLASSES, IMAGE_REALS), jnp.float32), jnp.zeros((CLASSES,), jnp.float32))
    inputs = (images.reshape(group_count, group_size, IMAGE_REALS), precision.reshape(group_count, group_size),
              rotation_offset.reshape(group_count, group_size), prior_blocks.reshape(group_count, N_DOM, CLASS_BLOCKS))
    (class_total, mass_total), evidence = lax.scan(one_group, initial, inputs)
    new_classes = (class_total + CLASS_PRIOR * classes.astype(jnp.float32)) / (mass_total + CLASS_PRIOR)[:, None]
    return new_classes, evidence.reshape(PARTICLES)
```

```python
import math

import jax
import jax.numpy as jnp
import numpy as np
from jax import lax
from jax.experimental import pallas as pl
from jax.experimental.pallas import tpu as pltpu
from jax.sharding import PartitionSpec as P

FREQUENCIES = 64
CYCLES = 32
PART = FREQUENCIES * CYCLES
ROTATIONS = 36
CLASS_BLOCK = 5
EXCLUDED = -1e30
PRIOR_WIDTH = 12.0
CLASS_PRIOR = 16.0

RESIDUES = 19
GROUP = 4
LANES = 128
OWN = 96
HALF_CLASSES = 50
HALF_ROWS = 56
ROWS = 2 * HALF_ROWS
COLS = 2 * LANES
CHUNKS = 64
BLOCKS = 32
SUM_SCALE = 0.25

MEMBERS = []
for _j in range(RESIDUES):
    _same = [(m, 1) for m in range(FREQUENCIES) if m % ROTATIONS == _j]
    _back = [(m, -1) for m in range(FREQUENCIES) if m % ROTATIONS == (ROTATIONS - _j) % ROTATIONS and _j not in (0, 18)]
    MEMBERS.append(_same + _back)


def cosv(k):
    return float(np.cos(2.0 * np.pi * (k % 36) / 36.0))


def sinv(k):
    return float(np.sin(2.0 * np.pi * (k % 36) / 36.0))


def lin(values, coefs):
    total = None
    for v, c in zip(values, coefs):
        if abs(c) < 1e-12:
            continue
        if abs(c - 1.0) < 1e-12:
            term = v
        elif abs(c + 1.0) < 1e-12:
            term = -v
        else:
            term = v * c
        total = term if total is None else total + term
    return total


def dft_cos18(x):
    even = [lin([x[j] for j in range(0, 10, 2)], [cosv(2 * j * r) for j in range(0, 10, 2)]) for r in range(5)]
    odd = [lin([x[j] for j in range(1, 10, 2)], [cosv(2 * j * r) for j in range(1, 10, 2)]) for r in range(5)]
    return [even[r] + odd[r] for r in range(5)] + [even[9 - r] - odd[9 - r] for r in range(5, 10)]


def dft_sin18(x):
    even = [lin([x[j] for j in range(2, 9, 2)], [sinv(2 * j * r) for j in range(2, 9, 2)]) for r in range(1, 5)]
    odd = [lin([x[j] for j in range(1, 9, 2)], [sinv(2 * j * r) for j in range(1, 9, 2)]) for r in range(1, 5)]
    return [None] + [odd[r] + even[r] for r in range(4)] + [odd[8 - r] - even[8 - r] for r in range(5, 9)]


def cos_sum(a):
    even = dft_cos18([a[2 * j] for j in range(10)])
    odds = [a[j] for j in range(1, 18, 2)]
    odd = [lin(odds, [cosv(j * r) for j in range(1, 18, 2)]) for r in range(9)]
    return [even[r] + odd[r] for r in range(9)] + [even[9]] + [even[18 - r] - odd[18 - r] for r in range(10, 19)]


def sin_sum(b):
    even = dft_sin18([None] + [b[2 * j] for j in range(1, 9)])
    odds = [b[j] for j in range(1, 18, 2)]
    odd = [None] + [lin(odds, [sinv(j * r) for j in range(1, 18, 2)]) for r in range(1, 10)]
    return [None] + [odd[r] + even[r] for r in range(1, 9)] + [odd[9]] + [odd[18 - r] - even[18 - r] for r in range(10, 18)]


def gather_lanes(ref, part, j):
    rows = ref.shape[0]
    pieces = [ref[:, part * PART + m * CYCLES : part * PART + (m + 1) * CYCLES] for m, _ in MEMBERS[j]]
    if len(pieces) < GROUP:
        pieces.append(jnp.zeros((rows, (GROUP - len(pieces)) * CYCLES), ref.dtype))
    return jnp.concatenate(pieces, axis=1)


def sign_lanes(j, rows, dtype):
    lane = lax.broadcasted_iota(jnp.int32, (rows, LANES), 1)
    same = sum(1 for _, s in MEMBERS[j] if s > 0) * CYCLES
    return jnp.where(lane < same, 1.0, -1.0).astype(dtype)


def score_kernel(own_ref, other_ref, cls_ref, prec_ref, offset_ref, admit_ref, w_ref, xp_ref, stat_ref, ab_ref, sc_ref, base_ref, prior_ref):
    zeros = jnp.zeros((LANES - OWN, RESIDUES * COLS), jnp.bfloat16)
    xp_ref[OWN:LANES] = zeros
    xp_ref[LANES + OWN :] = zeros
    for j in range(RESIDUES):
        for part in range(2):
            at = j * COLS + part * LANES
            xp_ref[0:OWN, at : at + LANES] = gather_lanes(own_ref, part, j)
            xp_ref[LANES : LANES + OWN, at : at + LANES] = gather_lanes(other_ref, part, j)
    for j in range(RESIDUES):
        c_re = gather_lanes(cls_ref, 0, j)
        c_im = gather_lanes(cls_ref, 1, j)
        lhs = jnp.concatenate([c_re, c_im], axis=1)
        if 0 < j < 18:
            sign = sign_lanes(j, ROWS, jnp.bfloat16)
            lhs = jnp.concatenate([lhs, jnp.concatenate([c_im * sign, -(c_re * sign)], axis=1)], axis=0)
        got = lax.dot_general(
            lhs, xp_ref[:, j * COLS : (j + 1) * COLS], (((1,), (1,)), ((), ())), preferred_element_type=jnp.float32
        )
        ab_ref[j] = got[:ROWS]
        if 0 < j < 18:
            ab_ref[18 + j] = got[ROWS:]
    members = cls_ref[...].astype(jnp.float32)
    norm = jnp.sum(members * members, axis=1, keepdims=True)
    base_ref[...] = jnp.where(admit_ref[...] > 0.0, -0.5 * norm * prec_ref[...], EXCLUDED)
    steps = lax.rem(lax.broadcasted_iota(jnp.int32, (40, COLS), 0) - offset_ref[...] + ROTATIONS, ROTATIONS)
    distance = jnp.minimum(steps, ROTATIONS - steps).astype(jnp.float32) * (1.0 / PRIOR_WIDTH)
    prior_ref[...] = -0.5 * distance * distance

    for half in range(2):
        lanes = slice(half * LANES, (half + 1) * LANES)
        prec = jnp.broadcast_to(prec_ref[:, lanes], (8, LANES))

        def scores(i, peak):
            rows = pl.ds(pl.multiple_of(i * 8, 8), 8)
            a = [ab_ref[j, rows, lanes] for j in range(19)]
            b = [None] + [ab_ref[18 + j, rows, lanes] for j in range(1, 18)]
            base = base_ref[rows, lanes]
            c = cos_sum(a)
            s = sin_sum(b)
            for r in range(19):
                turned = [(r, c[r])] if r in (0, 18) else [(r, c[r] + s[r]), (36 - r, c[r] - s[r])]
                for turn, correlation in turned:
                    score = correlation * prec + (base + prior_ref[turn : turn + 1, lanes])
                    sc_ref[turn, rows, lanes] = score
                    peak = jnp.maximum(peak, score)
            return peak

        peak = lax.fori_loop(0, ROWS // 8, scores, jnp.full((8, LANES), EXCLUDED, jnp.float32))
        peak = jnp.broadcast_to(jnp.max(peak, axis=0, keepdims=True), (8, LANES))

        def weights(i, mass):
            rows = pl.ds(pl.multiple_of(i * 8, 8), 8)
            e = [jnp.exp(sc_ref[r, rows, lanes] - peak) for r in range(ROTATIONS)]
            both = [e[0]] + [e[r] + e[36 - r] for r in range(1, 18)] + [e[18]]
            diff = [None] + [e[r] - e[36 - r] for r in range(1, 18)]
            c = cos_sum(both)
            s = sin_sum(diff)
            for j in range(19):
                w_ref[j, rows, lanes] = c[j]
            for j in range(1, 18):
                w_ref[18 + j, rows, lanes] = s[j]
            return mass + c[0]

        mass = lax.fori_loop(0, ROWS // 8, weights, jnp.zeros((8, LANES), jnp.float32))
        stat_ref[0:8, lanes] = peak
        stat_ref[8:16, lanes] = jnp.broadcast_to(jnp.sum(mass, axis=0, keepdims=True), (8, LANES))


def sums_kernel(w_ref, xp_ref, mine_ref, theirs_ref, out_ref, evidence_ref, pc_ref):
    peak_a = mine_ref[0:1, :]
    mass_a = mine_ref[8:9, :]
    peak_b = jnp.concatenate([theirs_ref[0:1, LANES:], theirs_ref[0:1, :LANES]], axis=1)
    mass_b = jnp.concatenate([theirs_ref[8:9, LANES:], theirs_ref[8:9, :LANES]], axis=1)
    peak = jnp.maximum(peak_a, peak_b)
    lift = jnp.exp(peak_a - peak)
    mass = mass_a * lift + mass_b * jnp.exp(peak_b - peak)
    lane = lax.broadcasted_iota(jnp.int32, (1, COLS), 1)
    held = lax.rem(lane, LANES) < OWN
    mass = jnp.where(held, mass, 1.0)
    evidence_ref[...] = jnp.broadcast_to(peak + jnp.log(mass), (8, COLS))
    scale = jnp.where(held, lift / mass, 0.0)

    def split(value):
        scaled = value * scale
        high = scaled.astype(jnp.bfloat16)
        return high, (scaled - high.astype(jnp.float32)).astype(jnp.bfloat16)

    high, low = split(w_ref[0])
    ones = jnp.ones((8, COLS), jnp.bfloat16)
    dims = (((1,), (1,)), ((), ()))
    total = lax.dot_general(ones, high, dims, preferred_element_type=jnp.float32)
    total = total + lax.dot_general(ones, low, dims, preferred_element_type=jnp.float32)
    total = jnp.concatenate([total, jnp.zeros((8, LANES - ROWS), jnp.float32)], axis=1)[0:1]

    for j in range(RESIDUES):
        high, low = split(w_ref[j])
        if 0 < j < 18:
            high_s, low_s = split(w_ref[18 + j])
            high = jnp.concatenate([high, high_s], axis=0)
            low = jnp.concatenate([low, low_s], axis=0)
        images = xp_ref[:, j * COLS : (j + 1) * COLS]
        dims = (((1,), (0,)), ((), ()))
        got = lax.dot_general(high, images, dims, preferred_element_type=jnp.float32)
        got = got + lax.dot_general(low, images, dims, preferred_element_type=jnp.float32)
        re, im = got[:ROWS, :LANES], got[:ROWS, LANES:]
        if 0 < j < 18:
            sign = sign_lanes(j, ROWS, jnp.float32)
            re, im = re - sign * got[ROWS:, LANES:], im + sign * got[ROWS:, :LANES]
        pc_ref[:, j * COLS : j * COLS + LANES] = re * SUM_SCALE
        pc_ref[:, j * COLS + LANES : (j + 1) * COLS] = im * SUM_SCALE

    place = {}
    for j in range(RESIDUES):
        for at, (m, _) in enumerate(MEMBERS[j]):
            place[m] = j * COLS + at * CYCLES
    row = lax.broadcasted_iota(jnp.int32, (HALF_ROWS, LANES), 0)
    for block in range(BLOCKS):
        part, first = divmod(block, BLOCKS // 2)
        starts = [place[first * GROUP + q] + part * LANES for q in range(GROUP)]
        whole = jnp.concatenate([pc_ref[:, at : at + CYCLES] for at in starts], axis=1)
        for half in range(2):
            rows = whole[half * HALF_ROWS : (half + 1) * HALF_ROWS]
            out_ref[half * BLOCKS + block] = jnp.where(row == HALF_CLASSES, total * SUM_SCALE, rows)


def finish_kernel(half_ref, sum_ref, cls_ref, out_ref):
    total = sum_ref[HALF_CLASSES : HALF_CLASSES + 1, :]
    row = lax.broadcasted_iota(jnp.int32, (HALF_ROWS, LANES), 0)
    lane = lax.broadcasted_iota(jnp.int32, (HALF_ROWS, LANES), 1)
    weight = jnp.sum(jnp.where(lane == row + half_ref[0] * HALF_ROWS, total, 0.0), axis=1, keepdims=True)
    whole = sum_ref[...] * (1.0 / SUM_SCALE) + CLASS_PRIOR * cls_ref[...]
    out_ref[...] = whole / (weight * (1.0 / SUM_SCALE) + CLASS_PRIOR)


VMEM = pl.BlockSpec(memory_space=pltpu.VMEM)
SMEM = pl.BlockSpec(memory_space=pltpu.SMEM)


def pad_lanes(own, other):
    pad = jnp.zeros((LANES - OWN,), own.dtype)
    return jnp.concatenate([own, pad, other, pad])[None, :]


def shards(images, precision, rotation_offset, classes, prior_blocks):
    swap = [(0, 1), (1, 0)]
    other_images = lax.ppermute(images, "dom", swap)
    small = jnp.stack([precision, rotation_offset.astype(jnp.bfloat16)])
    other_small = lax.ppermute(small, "dom", swap)
    prec = pad_lanes(precision.astype(jnp.float32), other_small[0].astype(jnp.float32))
    offsets = pad_lanes(rotation_offset, other_small[1].astype(jnp.int32))

    dom = lax.axis_index("dom")
    mask_rows = jnp.stack([prior_blocks[dom], prior_blocks[1 - dom]])
    by_class = jnp.repeat(mask_rows, CLASS_BLOCK, axis=1).reshape(2, 2, HALF_CLASSES)
    by_class = jnp.pad(by_class, ((0, 0), (0, 0), (0, HALF_ROWS - HALF_CLASSES))).reshape(2, ROWS)
    admit = jnp.repeat((by_class == 1).astype(jnp.float32).T, LANES, axis=1)
    halves = jnp.pad(classes.reshape(2, HALF_CLASSES, -1), ((0, 0), (0, HALF_ROWS - HALF_CLASSES), (0, 0)))
    padded = halves.reshape(ROWS, -1)

    weights, by_residue, mine = pl.pallas_call(
        score_kernel,
        out_shape=(
            jax.ShapeDtypeStruct((36, ROWS, COLS), jnp.float32),
            jax.ShapeDtypeStruct((COLS, RESIDUES * COLS), jnp.bfloat16),
            jax.ShapeDtypeStruct((16, COLS), jnp.float32),
        ),
        in_specs=[VMEM] * 6,
        out_specs=(VMEM, VMEM, VMEM),
        scratch_shapes=[
            pltpu.VMEM((36, ROWS, COLS), jnp.float32),
            pltpu.VMEM((36, ROWS, COLS), jnp.float32),
            pltpu.VMEM((ROWS, COLS), jnp.float32),
            pltpu.VMEM((40, COLS), jnp.float32),
        ],
        compiler_params=pltpu.CompilerParams(vmem_limit_bytes=48 * 1024 * 1024),
        name="score",
    )(images, other_images, padded, prec, offsets, admit)

    theirs = lax.ppermute(mine, "dom", swap)

    parts, evidence = pl.pallas_call(
        sums_kernel,
        out_shape=(
            jax.ShapeDtypeStruct((CHUNKS, HALF_ROWS, LANES), jnp.float32),
            jax.ShapeDtypeStruct((8, COLS), jnp.float32),
        ),
        in_specs=[VMEM] * 4,
        out_specs=(VMEM, VMEM),
        scratch_shapes=[pltpu.VMEM((ROWS, RESIDUES * COLS), jnp.float32)],
        compiler_params=pltpu.CompilerParams(vmem_limit_bytes=48 * 1024 * 1024),
        name="sums",
    )(weights, by_residue, mine, theirs)

    got = lax.all_to_all(parts.astype(jnp.float16), "cls", 0, 0, tiled=True)
    total = jnp.sum(got.astype(jnp.float32), axis=0)
    cls = lax.axis_index("cls")
    half, block = cls // BLOCKS, cls % BLOCKS
    chunk = lax.dynamic_slice(halves, (half, 0, block * LANES), (1, HALF_ROWS, LANES))[0].astype(jnp.float32)
    new_chunk = pl.pallas_call(
        finish_kernel,
        out_shape=jax.ShapeDtypeStruct((HALF_ROWS, LANES), jnp.float32),
        in_specs=[SMEM, VMEM, VMEM],
        out_specs=VMEM,
        name="finish",
    )(half.astype(jnp.int32).reshape(1), total, chunk)
    repeated = jnp.broadcast_to(new_chunk.astype(jnp.float16)[None], (CHUNKS, HALF_ROWS, LANES))
    whole = lax.all_to_all(repeated, "cls", 0, 0, tiled=True)
    whole = whole.astype(jnp.float32).reshape(2, BLOCKS, HALF_ROWS, LANES)[:, :, :HALF_CLASSES]
    new_classes = whole.transpose(0, 2, 1, 3).reshape(2 * HALF_CLASSES, -1)
    return new_classes, evidence[0, :OWN]


def solution(mesh):
    in_specs = (
        P(("cls", "dom"), None),
        P(("cls", "dom")),
        P(("cls", "dom")),
        P("dom", None),
        P("cls", "dom"),
    )
    out_specs = (P("dom", None), P(("cls", "dom")))
    return jax.shard_map(shards, mesh=mesh, in_specs=in_specs, out_specs=out_specs, check_vma=False)
```

```python
import math

import jax
import jax.numpy as jnp
import numpy as np
from jax import lax
from jax.experimental import pallas as pl
from jax.experimental.pallas import tpu as pltpu
from jax.sharding import PartitionSpec as P

FREQUENCIES = 64
CYCLES = 32
PART = FREQUENCIES * CYCLES
ROTATIONS = 36
CLASS_BLOCK = 5
EXCLUDED = -1e30
PRIOR_WIDTH = 12.0
CLASS_PRIOR = 16.0

RESIDUES = 19
GROUP = 4
LANES = 128
OWN = 96
CLASSES = 100
ROWS = 104
SPLIT = 48
HALF_ROWS = 56
TOTAL_ROW = 52
COLS = 2 * LANES
CHUNKS = 64
BLOCKS = 32
SUM_SCALE = 0.25

MEMBERS = []
for _j in range(RESIDUES):
    _same = [(m, 1) for m in range(FREQUENCIES) if m % ROTATIONS == _j]
    _back = [(m, -1) for m in range(FREQUENCIES) if m % ROTATIONS == (ROTATIONS - _j) % ROTATIONS and _j not in (0, 18)]
    MEMBERS.append(_same + _back)


def cosv(k):
    return float(np.cos(2.0 * np.pi * (k % 36) / 36.0))


def sinv(k):
    return float(np.sin(2.0 * np.pi * (k % 36) / 36.0))


def lin(values, coefs):
    total = None
    for v, c in zip(values, coefs):
        if abs(c) < 1e-12:
            continue
        if abs(c - 1.0) < 1e-12:
            term = v
        elif abs(c + 1.0) < 1e-12:
            term = -v
        else:
            term = v * c
        total = term if total is None else total + term
    return total


def dft_cos18(x):
    even = [lin([x[j] for j in range(0, 10, 2)], [cosv(2 * j * r) for j in range(0, 10, 2)]) for r in range(5)]
    odd = [lin([x[j] for j in range(1, 10, 2)], [cosv(2 * j * r) for j in range(1, 10, 2)]) for r in range(5)]
    return [even[r] + odd[r] for r in range(5)] + [even[9 - r] - odd[9 - r] for r in range(5, 10)]


def dft_sin18(x):
    even = [lin([x[j] for j in range(2, 9, 2)], [sinv(2 * j * r) for j in range(2, 9, 2)]) for r in range(1, 5)]
    odd = [lin([x[j] for j in range(1, 9, 2)], [sinv(2 * j * r) for j in range(1, 9, 2)]) for r in range(1, 5)]
    return [None] + [odd[r] + even[r] for r in range(4)] + [odd[8 - r] - even[8 - r] for r in range(5, 9)]


def cos_sum(a):
    even = dft_cos18([a[2 * j] for j in range(10)])
    odds = [a[j] for j in range(1, 18, 2)]
    odd = [lin(odds, [cosv(j * r) for j in range(1, 18, 2)]) for r in range(9)]
    return [even[r] + odd[r] for r in range(9)] + [even[9]] + [even[18 - r] - odd[18 - r] for r in range(10, 19)]


def sin_sum(b):
    even = dft_sin18([None] + [b[2 * j] for j in range(1, 9)])
    odds = [b[j] for j in range(1, 18, 2)]
    odd = [None] + [lin(odds, [sinv(j * r) for j in range(1, 18, 2)]) for r in range(1, 10)]
    return [None] + [odd[r] + even[r] for r in range(1, 9)] + [odd[9]] + [odd[18 - r] - even[18 - r] for r in range(10, 18)]


def gather_lanes(ref, part, j):
    rows = ref.shape[0]
    pieces = [ref[:, part * PART + m * CYCLES : part * PART + (m + 1) * CYCLES] for m, _ in MEMBERS[j]]
    if len(pieces) < GROUP:
        pieces.append(jnp.zeros((rows, (GROUP - len(pieces)) * CYCLES), ref.dtype))
    return jnp.concatenate(pieces, axis=1)


def sign_lanes(j, rows):
    lane = lax.broadcasted_iota(jnp.int32, (rows, LANES), 1)
    same = sum(1 for _, s in MEMBERS[j] if s > 0) * CYCLES
    return jnp.where(lane < same, 1.0, -1.0)


def particle_row(values):
    return jnp.concatenate([values, jnp.zeros((1, LANES - OWN), values.dtype)], axis=1)


def arrange_classes(cls_ref, cp_ref, norm_ref):
    zeros = jnp.zeros((ROWS - CLASSES, COLS), jnp.float32)
    norm = jnp.zeros((CLASSES, LANES), jnp.float32)
    for j in range(RESIDUES):
        c_re = gather_lanes(cls_ref, 0, j).astype(jnp.float32)
        c_im = gather_lanes(cls_ref, 1, j).astype(jnp.float32)
        norm = norm + c_re * c_re + c_im * c_im
        cosine = jnp.concatenate([jnp.concatenate([c_re, c_im], axis=1), zeros], axis=0)
        if 0 < j < 18:
            sign = sign_lanes(j, CLASSES)
            sine = jnp.concatenate([jnp.concatenate([c_im * sign, -(c_re * sign)], axis=1), zeros], axis=0)
        else:
            sine = jnp.zeros((ROWS, COLS), jnp.float32)
        cp_ref[j] = jnp.concatenate([cosine, sine], axis=0).astype(jnp.bfloat16)
    norm = jnp.broadcast_to(jnp.sum(norm, axis=1, keepdims=True), (CLASSES, LANES))
    norm_ref[...] = jnp.concatenate([norm, jnp.zeros((ROWS - CLASSES, LANES), jnp.float32)], axis=0)


def score_block(blocks_ref, block_row, image_ref, precision, offset, cp_ref, norm_ref, w_ref, xp_ref, stat_ref, ab_ref, sc_ref, base_ref, prior_ref):
    row = lax.broadcasted_iota(jnp.int32, (ROWS, LANES), 0)
    admit = jnp.zeros((ROWS, LANES), jnp.int32)
    for block in range(CLASSES // CLASS_BLOCK):
        inside = (row >= block * CLASS_BLOCK) & (row < (block + 1) * CLASS_BLOCK)
        admit = jnp.where(inside, blocks_ref[block_row, block], admit)
    base_ref[...] = jnp.where(admit == 1, -0.5 * norm_ref[...] * precision, EXCLUDED)
    steps = lax.rem(lax.broadcasted_iota(jnp.int32, (40, LANES), 0) - offset + ROTATIONS, ROTATIONS)
    distance = jnp.minimum(steps, ROTATIONS - steps).astype(jnp.float32) * (1.0 / PRIOR_WIDTH)
    prior_ref[...] = -0.5 * distance * distance
    xp_ref[OWN:LANES] = jnp.zeros((LANES - OWN, RESIDUES * COLS), jnp.bfloat16)
    for j in range(RESIDUES):
        for part in range(2):
            at = j * COLS + part * LANES
            xp_ref[0:OWN, at : at + LANES] = gather_lanes(image_ref, part, j)
        got = lax.dot_general(
            cp_ref[j], xp_ref[:, j * COLS : (j + 1) * COLS], (((1,), (1,)), ((), ())), preferred_element_type=jnp.float32
        )
        ab_ref[j] = got[:ROWS]
        if 0 < j < 18:
            ab_ref[18 + j] = got[ROWS:]

    prec = jnp.broadcast_to(precision, (8, LANES))

    def scores(i, peak):
        rows = pl.ds(pl.multiple_of(i * 8, 8), 8)
        a = [ab_ref[j, rows] for j in range(19)]
        b = [None] + [ab_ref[18 + j, rows] for j in range(1, 18)]
        base = base_ref[rows]
        c = cos_sum(a)
        s = sin_sum(b)
        for r in range(19):
            turned = [(r, c[r])] if r in (0, 18) else [(r, c[r] + s[r]), (36 - r, c[r] - s[r])]
            for turn, correlation in turned:
                score = correlation * prec + (base + prior_ref[turn : turn + 1])
                sc_ref[turn, rows] = score
                peak = jnp.maximum(peak, score)
        return peak

    peak = lax.fori_loop(0, ROWS // 8, scores, jnp.full((8, LANES), EXCLUDED, jnp.float32), unroll=True)
    peak = jnp.broadcast_to(jnp.max(peak, axis=0, keepdims=True), (8, LANES))

    def weights(i, mass):
        rows = pl.ds(pl.multiple_of(i * 8, 8), 8)
        e = [jnp.exp(sc_ref[r, rows] - peak) for r in range(ROTATIONS)]
        both = [e[0]] + [e[r] + e[36 - r] for r in range(1, 18)] + [e[18]]
        diff = [None] + [e[r] - e[36 - r] for r in range(1, 18)]
        c = cos_sum(both)
        s = sin_sum(diff)
        for j in range(19):
            w_ref[j, rows] = c[j]
        for j in range(1, 18):
            w_ref[18 + j, rows] = s[j]
        return mass + c[0]

    mass = lax.fori_loop(0, ROWS // 8, weights, jnp.zeros((8, LANES), jnp.float32), unroll=True)
    stat_ref[0:8] = peak
    stat_ref[8:16] = jnp.broadcast_to(jnp.sum(mass, axis=0, keepdims=True), (8, LANES))


def class_kernel(cls_ref, cp_ref, norm_ref):
    arrange_classes(cls_ref, cp_ref, norm_ref)


def own_kernel(blocks_ref, image_ref, prec_ref, offset_ref, cp_ref, norm_ref, w_ref, xp_ref, stat_ref, *scratch):
    precision = particle_row(prec_ref[...].astype(jnp.float32))
    offset = particle_row(offset_ref[...])
    score_block(blocks_ref, lax.axis_index("dom"), image_ref, precision, offset, cp_ref, norm_ref, w_ref, xp_ref, stat_ref, *scratch)


def other_kernel(blocks_ref, image_ref, prec_ref, offset_ref, cp_ref, norm_ref, stat_a, w_ref, xp_ref, stats_ref, *scratch):
    precision = particle_row(prec_ref[...].astype(jnp.float32))
    offset = particle_row(offset_ref[...])
    score_block(blocks_ref, 1 - lax.axis_index("dom"), image_ref, precision, offset, cp_ref, norm_ref, w_ref, xp_ref, stats_ref.at[1], *scratch)
    stats_ref[0] = stat_a[...]


def sums_kernel(w_a, w_b, xp_a, xp_b, mine, theirs, out_ref, evidence_ref, pc_ref):
    held = lax.broadcasted_iota(jnp.int32, (1, LANES), 1) < OWN

    def settle(mine, theirs):
        peak = jnp.maximum(mine[0:1], theirs[0:1])
        lift = jnp.exp(mine[0:1] - peak)
        mass = mine[8:9] * lift + theirs[8:9] * jnp.exp(theirs[0:1] - peak)
        mass = jnp.where(held, mass, 1.0)
        return jnp.where(held, lift / mass, 0.0), peak + jnp.log(mass)

    scale_a, evidence = settle(mine[0], theirs[1])
    scale_b, _ = settle(mine[1], theirs[0])
    evidence_ref[...] = jnp.broadcast_to(evidence, (8, LANES))

    def weights_of(i):
        return jnp.concatenate([w_a[i] * scale_a, w_b[i] * scale_b], axis=1)

    totals = weights_of(0)
    totals = jnp.concatenate([totals, jnp.zeros((LANES - ROWS, COLS), jnp.float32)], axis=0)
    high = totals.astype(jnp.bfloat16)
    low = (totals - high.astype(jnp.float32)).astype(jnp.bfloat16)
    ones = jnp.ones((16, COLS), jnp.bfloat16)
    dims = (((1,), (1,)), ((), ()))
    total = lax.dot_general(ones, high, dims, preferred_element_type=jnp.float32)
    total = total + lax.dot_general(ones, low, dims, preferred_element_type=jnp.float32)
    total = total[0:1]

    for j in range(RESIDUES):
        pair = 0 < j < 18
        weight = weights_of(j)
        if pair:
            weight = jnp.concatenate([weight, weights_of(18 + j)], axis=0)
        else:
            weight = jnp.concatenate([weight, jnp.zeros((8, COLS), jnp.float32)], axis=0)
        high = weight.astype(jnp.bfloat16)
        low = (weight - high.astype(jnp.float32)).astype(jnp.bfloat16)
        lanes = slice(j * COLS, (j + 1) * COLS)
        images = jnp.concatenate([xp_a[:, lanes], xp_b[:, lanes]], axis=0)
        dims = (((1,), (0,)), ((), ()))
        got = lax.dot_general(high, images, dims, preferred_element_type=jnp.float32)
        got = got + lax.dot_general(low, images, dims, preferred_element_type=jnp.float32)
        re, im = got[:ROWS, :LANES], got[:ROWS, LANES:]
        if pair:
            sign = sign_lanes(j, ROWS)
            re, im = re - sign * got[ROWS:, LANES:], im + sign * got[ROWS:, :LANES]
        pc_ref[:, j * COLS : j * COLS + LANES] = re * SUM_SCALE
        pc_ref[:, j * COLS + LANES : (j + 1) * COLS] = im * SUM_SCALE

    place = {}
    for j in range(RESIDUES):
        for at, (m, _) in enumerate(MEMBERS[j]):
            place[m] = j * COLS + at * CYCLES
    row = lax.broadcasted_iota(jnp.int32, (HALF_ROWS, LANES), 0)
    for block in range(BLOCKS):
        part, first = divmod(block, BLOCKS // 2)
        starts = [place[first * GROUP + q] + part * LANES for q in range(GROUP)]
        whole = jnp.concatenate([pc_ref[:, at : at + CYCLES] for at in starts], axis=1)
        for half in range(2):
            rows = whole[half * SPLIT : half * SPLIT + HALF_ROWS]
            out_ref[half * BLOCKS + block] = jnp.where(row == TOTAL_ROW, total * SUM_SCALE, rows)


FINISH_STEPS = 4
STEP_BLOCKS = BLOCKS // FINISH_STEPS


def finish_kernel(sum_ref, cls_hbm, out_hbm, cls_ref, out_ref, cls_sem, out_sems):
    fetch = pltpu.make_async_copy(cls_hbm, cls_ref, cls_sem)
    fetch.start()
    row = lax.broadcasted_iota(jnp.int32, (HALF_ROWS, LANES), 0)
    lane = lax.broadcasted_iota(jnp.int32, (HALF_ROWS, LANES), 1)
    share = []
    for half in range(2):
        total = sum_ref[half, 0, TOTAL_ROW : TOTAL_ROW + 1, :]
        weight = jnp.sum(jnp.where(lane == row + half * SPLIT, total, 0.0), axis=1, keepdims=True)
        share.append(1.0 / (weight * (1.0 / SUM_SCALE) + CLASS_PRIOR))
    fetch.wait()
    copies = []
    for step in range(FINISH_STEPS):
        for block in range(step * STEP_BLOCKS, (step + 1) * STEP_BLOCKS):
            lanes = slice(block * LANES, (block + 1) * LANES)
            old = cls_ref[:, lanes].astype(jnp.float32)
            for half in range(2):
                count = SPLIT if half == 0 else CLASSES - SPLIT
                rows = slice(half * SPLIT, half * SPLIT + count)
                new = sum_ref[half, block, 0:count] * (1.0 / SUM_SCALE) + CLASS_PRIOR * old[rows]
                out_ref[rows, lanes] = new * share[half][:count]
        lanes = slice(step * STEP_BLOCKS * LANES, (step + 1) * STEP_BLOCKS * LANES)
        copy = pltpu.make_async_copy(out_ref.at[:, lanes], out_hbm.at[:, lanes], out_sems.at[step])
        copy.start()
        copies.append(copy)
    for copy in copies:
        copy.wait()


VMEM = pl.BlockSpec(memory_space=pltpu.VMEM)
SMEM = pl.BlockSpec(memory_space=pltpu.SMEM)


ANY = pl.BlockSpec(memory_space=pl.ANY)
MIB = 1024 * 1024


def shards(images, precision, rotation_offset, classes, prior_blocks):
    swap = [(0, 1), (1, 0)]
    other_images = lax.ppermute(images, "dom", swap)
    other_precision = lax.ppermute(precision, "dom", swap)
    other_offset = lax.ppermute(rotation_offset, "dom", swap)

    block_out = (
        jax.ShapeDtypeStruct((36, ROWS, LANES), jnp.float32),
        jax.ShapeDtypeStruct((LANES, RESIDUES * COLS), jnp.bfloat16),
    )
    class_out = (
        jax.ShapeDtypeStruct((RESIDUES, 2 * ROWS, COLS), jnp.bfloat16),
        jax.ShapeDtypeStruct((ROWS, LANES), jnp.float32),
    )
    block_scratch = [
        pltpu.VMEM((36, ROWS, LANES), jnp.float32),
        pltpu.VMEM((36, ROWS, LANES), jnp.float32),
        pltpu.VMEM((ROWS, LANES), jnp.float32),
        pltpu.VMEM((40, LANES), jnp.float32),
    ]
    cost = pl.CostEstimate(flops=4 * 10**9, bytes_accessed=8 * MIB, transcendentals=36 * 104 * 128)

    cp, norm = pl.pallas_call(
        class_kernel,
        out_shape=class_out,
        in_specs=[VMEM],
        out_specs=(VMEM,) * 2,
        compiler_params=pltpu.CompilerParams(vmem_limit_bytes=12 * MIB),
        cost_estimate=cost,
        name="classes",
    )(classes)

    w_a, xp_a, stat_a = pl.pallas_call(
        own_kernel,
        out_shape=block_out + (jax.ShapeDtypeStruct((16, LANES), jnp.float32),),
        in_specs=[SMEM] + [VMEM] * 5,
        out_specs=(VMEM,) * 3,
        scratch_shapes=block_scratch,
        compiler_params=pltpu.CompilerParams(vmem_limit_bytes=20 * MIB),
        cost_estimate=cost,
        name="own_scores",
    )(prior_blocks, images, precision.reshape(1, OWN), rotation_offset.reshape(1, OWN), cp, norm)

    w_b, xp_b, mine = pl.pallas_call(
        other_kernel,
        out_shape=block_out + (jax.ShapeDtypeStruct((2, 16, LANES), jnp.float32),),
        in_specs=[SMEM] + [VMEM] * 6,
        out_specs=(VMEM,) * 3,
        scratch_shapes=block_scratch,
        compiler_params=pltpu.CompilerParams(vmem_limit_bytes=20 * MIB),
        cost_estimate=cost,
        name="other_scores",
    )(prior_blocks, other_images, other_precision.reshape(1, OWN), other_offset.reshape(1, OWN), cp, norm, stat_a)
    theirs = lax.ppermute(mine, "dom", swap)

    parts, evidence = pl.pallas_call(
        sums_kernel,
        out_shape=(
            jax.ShapeDtypeStruct((CHUNKS, HALF_ROWS, LANES), jnp.float32),
            jax.ShapeDtypeStruct((8, LANES), jnp.float32),
        ),
        in_specs=[VMEM] * 6,
        out_specs=(VMEM, VMEM),
        scratch_shapes=[pltpu.VMEM((ROWS, RESIDUES * COLS), jnp.float32)],
        compiler_params=pltpu.CompilerParams(vmem_limit_bytes=20 * MIB),
        name="sums",
    )(w_a, w_b, xp_a, xp_b, mine, theirs)

    got = lax.all_to_all(parts.astype(jnp.float16), "cls", 0, 0, tiled=True)
    total = jnp.sum(got.astype(jnp.float32), axis=0).astype(jnp.float16)
    repeated = jnp.broadcast_to(total[None], (CHUNKS, HALF_ROWS, LANES))
    whole = lax.all_to_all(repeated, "cls", 0, 0, tiled=True)
    new_classes = pl.pallas_call(
        finish_kernel,
        out_shape=jax.ShapeDtypeStruct((CLASSES, BLOCKS * LANES), jnp.float32),
        in_specs=[VMEM, ANY],
        out_specs=ANY,
        scratch_shapes=[
            pltpu.VMEM(classes.shape, jnp.bfloat16),
            pltpu.VMEM((CLASSES, BLOCKS * LANES), jnp.float32),
            pltpu.SemaphoreType.DMA,
            pltpu.SemaphoreType.DMA((FINISH_STEPS,)),
        ],
        compiler_params=pltpu.CompilerParams(vmem_limit_bytes=12 * MIB),
        name="finish",
    )(whole.astype(jnp.float32).reshape(2, BLOCKS, HALF_ROWS, LANES), classes)
    return new_classes, evidence[0, :OWN]


def solution(mesh):
    in_specs = (
        P(("cls", "dom"), None),
        P(("cls", "dom")),
        P(("cls", "dom")),
        P("dom", None),
        P("cls", "dom"),
    )
    out_specs = (P("dom", None), P(("cls", "dom")))
    return jax.shard_map(shards, mesh=mesh, in_specs=in_specs, out_specs=out_specs, check_vma=False)
```

```python
import math

import jax
import jax.numpy as jnp
import numpy as np
from jax import lax
from jax.experimental import pallas as pl
from jax.experimental.pallas import tpu as pltpu
from jax.sharding import PartitionSpec as P

FREQUENCIES = 64
CYCLES = 32
PART = FREQUENCIES * CYCLES
ROTATIONS = 36
CLASS_BLOCK = 5
EXCLUDED = -1e30
PRIOR_WIDTH = 12.0
CLASS_PRIOR = 16.0

RESIDUES = 19
GROUP = 4
LANES = 128
OWN = 96
CLASSES = 100
ROWS = 104
SPLIT = 48
HALF_ROWS = 56
TOTAL_ROW = 52
COLS = 2 * LANES
CHUNKS = 64
BLOCKS = 32
SUM_SCALE = 0.25

MEMBERS = []
for _j in range(RESIDUES):
    _same = [(m, 1) for m in range(FREQUENCIES) if m % ROTATIONS == _j]
    _back = [(m, -1) for m in range(FREQUENCIES) if m % ROTATIONS == (ROTATIONS - _j) % ROTATIONS and _j not in (0, 18)]
    MEMBERS.append(_same + _back)


def cosine(k):
    return float(np.cos(2.0 * np.pi * k / 9.0))


def sine(k):
    return float(np.sin(2.0 * np.pi * k / 9.0))


def nine_cos(x):
    c1, c2 = cosine(1), cosine(2)
    t, u = x[0] + x[3], (x[1] + x[2]) + x[4]
    base = x[0] - 0.5 * x[3]
    p, q = x[1] - x[4], x[2] - x[4]
    y1 = base + (p * c1 + q * c2)
    y2 = base + ((p - q) * c2 - q * c1)
    y4 = base - ((p - q) * c1 + p * c2)
    return [t + u, y1, y2, t - 0.5 * u, y4]


def nine_sin(x):
    s1, s3, s4 = sine(1), sine(3), sine(4)
    p, q = x[1] + x[2], x[2] + x[4]
    d = p - q
    t = x[3] * s3
    return [None, t + (p * s1 + q * s4), (d * s1 + p * s4) - t, ((x[1] - x[2]) + x[4]) * s3, t + (d * s4 - q * s1)]


def fold(j):
    j %= ROTATIONS
    return (j, 1) if j <= 18 else (ROTATIONS - j, -1)


def signed(values, j):
    at, sign = fold(j)
    return values[at] if sign > 0 else -values[at]


def rotation_of(r4, r9):
    return next(r for r in range(ROTATIONS) if r % 4 == r4 and r % 9 == r9)


def to_rotations(a, b):
    one = ([a[0]] + [a[fold(4 * k)[0]] for k in range(1, 5)], [None] + [signed(b, 4 * k) for k in range(1, 5)])
    alt = ([a[18]] + [a[fold(18 + 4 * k)[0]] for k in range(1, 5)], [None] + [signed(b, 18 + 4 * k) for k in range(1, 5)])
    cc, cs, sc, ss = [a[9]], [None], [b[9]], [None]
    for k in range(1, 5):
        a_p, b_p = a[fold(9 + 4 * k)[0]], b[fold(9 + 4 * k)[0]]
        a_m, b_m = a[fold(9 - 4 * k)[0]], b[fold(9 - 4 * k)[0]]
        assert fold(9 + 4 * k)[1] == fold(9 - 4 * k)[1]
        cc.append(a_p + a_m)
        ss.append(a_m - a_p)
        if fold(9 + 4 * k)[1] > 0:
            sc.append(b_p + b_m)
            cs.append(b_p - b_m)
        else:
            sc.append(-(b_p + b_m))
            cs.append(b_m - b_p)
    lines = []
    for even, odd in (one, alt, (cc, cs), (sc, ss)):
        e, o = nine_cos(even), nine_sin(odd)
        lines.append([e[0]] + [e[r] + o[r] for r in range(1, 5)] + [e[9 - r] - o[9 - r] for r in range(5, 9)])
    y = [None] * ROTATIONS
    for r9 in range(9):
        g1, gm, gc, gs = (line[r9] for line in lines)
        plus, minus = g1 + gm, g1 - gm
        y[rotation_of(0, r9)] = plus + gc
        y[rotation_of(2, r9)] = plus - gc
        y[rotation_of(1, r9)] = minus + gs
        y[rotation_of(3, r9)] = minus - gs
    return y


def from_rotations(e):
    lines = [[], [], [], []]
    for r9 in range(9):
        e0, e1, e2, e3 = (e[rotation_of(r4, r9)] for r4 in range(4))
        p, q = e0 + e2, e1 + e3
        for line, value in zip(lines, (p + q, p - q, e0 - e2, e1 - e3)):
            line.append(value)
    spectra = []
    for h in lines:
        even = [h[0]] + [h[k] + h[9 - k] for k in range(1, 5)]
        odd = [None] + [h[k] - h[9 - k] for k in range(1, 5)]
        spectra.append((nine_cos(even), nine_sin(odd)))
    (one_c, one_s), (alt_c, alt_s), (cc, cs), (sc, ss) = spectra
    c, s = [None] * RESIDUES, [None] * RESIDUES
    c[0], c[18], c[9], s[9] = one_c[0], alt_c[0], cc[0], sc[0]
    for k in range(1, 5):
        for first, cosines, sines in ((0, one_c, one_s), (18, alt_c, alt_s)):
            at, sign = fold(first + 4 * k)
            c[at], s[at] = cosines[k], sines[k] if sign > 0 else -sines[k]
        at_p, sign = fold(9 + 4 * k)
        at_m, _ = fold(9 - 4 * k)
        c[at_p], c[at_m] = cc[k] - ss[k], cc[k] + ss[k]
        if sign > 0:
            s[at_p], s[at_m] = sc[k] + cs[k], sc[k] - cs[k]
        else:
            s[at_p], s[at_m] = -(sc[k] + cs[k]), cs[k] - sc[k]
    return c, s


def gather_lanes(ref, part, j):
    rows = ref.shape[0]
    pieces = [ref[:, part * PART + m * CYCLES : part * PART + (m + 1) * CYCLES] for m, _ in MEMBERS[j]]
    if len(pieces) < GROUP:
        pieces.append(jnp.zeros((rows, (GROUP - len(pieces)) * CYCLES), ref.dtype))
    return jnp.concatenate(pieces, axis=1)


def sign_lanes(j, rows):
    lane = lax.broadcasted_iota(jnp.int32, (rows, LANES), 1)
    same = sum(1 for _, s in MEMBERS[j] if s > 0) * CYCLES
    return jnp.where(lane < same, 1.0, -1.0)


def particle_row(values):
    return jnp.concatenate([values, jnp.zeros((1, LANES - OWN), values.dtype)], axis=1)


def arrange_classes(cls_ref, cp_ref, norm_ref):
    zeros = jnp.zeros((ROWS - CLASSES, COLS), jnp.float32)
    norm = jnp.zeros((CLASSES, LANES), jnp.float32)
    for j in range(RESIDUES):
        c_re = gather_lanes(cls_ref, 0, j).astype(jnp.float32)
        c_im = gather_lanes(cls_ref, 1, j).astype(jnp.float32)
        norm = norm + c_re * c_re + c_im * c_im
        cosine = jnp.concatenate([jnp.concatenate([c_re, c_im], axis=1), zeros], axis=0)
        if 0 < j < 18:
            sign = sign_lanes(j, CLASSES)
            sine = jnp.concatenate([jnp.concatenate([c_im * sign, -(c_re * sign)], axis=1), zeros], axis=0)
        else:
            sine = jnp.zeros((ROWS, COLS), jnp.float32)
        cp_ref[j] = jnp.concatenate([cosine, sine], axis=0).astype(jnp.bfloat16)
    norm = jnp.broadcast_to(jnp.sum(norm, axis=1, keepdims=True), (CLASSES, LANES))
    norm_ref[...] = jnp.concatenate([norm, jnp.zeros((ROWS - CLASSES, LANES), jnp.float32)], axis=0)


def score_kernel(blocks_ref, own_ref, other_ref, prec_a, prec_b, offset_a, offset_b, cp_ref, norm_ref, e_ref, xp_ref, stat_ref, ab_ref, base_ref, prior_ref):
    row = lax.broadcasted_iota(jnp.int32, (ROWS, LANES), 0)
    dom = lax.axis_index("dom")
    precisions = [particle_row(p[...].astype(jnp.float32)) for p in (prec_a, prec_b)]
    for half in range(2):
        lanes = slice(half * LANES, (half + 1) * LANES)
        block_row = dom if half == 0 else 1 - dom
        admit = jnp.zeros((ROWS, LANES), jnp.int32)
        for block in range(CLASSES // CLASS_BLOCK):
            inside = (row >= block * CLASS_BLOCK) & (row < (block + 1) * CLASS_BLOCK)
            admit = jnp.where(inside, blocks_ref[block_row, block], admit)
        base_ref[:, lanes] = jnp.where(admit == 1, -0.5 * norm_ref[...] * precisions[half], EXCLUDED)
        offset = particle_row((offset_a, offset_b)[half][...])
        steps = lax.rem(lax.broadcasted_iota(jnp.int32, (40, LANES), 0) - offset + ROTATIONS, ROTATIONS)
        distance = jnp.minimum(steps, ROTATIONS - steps).astype(jnp.float32) * (1.0 / PRIOR_WIDTH)
        prior_ref[:, lanes] = -0.5 * distance * distance
    zeros = jnp.zeros((LANES - OWN, RESIDUES * COLS), jnp.bfloat16)
    xp_ref[OWN:LANES] = zeros
    xp_ref[LANES + OWN :] = zeros
    for j in range(RESIDUES):
        for part in range(2):
            at = j * COLS + part * LANES
            xp_ref[0:OWN, at : at + LANES] = gather_lanes(own_ref, part, j)
            xp_ref[LANES : LANES + OWN, at : at + LANES] = gather_lanes(other_ref, part, j)
        got = lax.dot_general(
            cp_ref[j], xp_ref[:, j * COLS : (j + 1) * COLS], (((1,), (1,)), ((), ())), preferred_element_type=jnp.float32
        )
        ab_ref[j] = got[:ROWS]
        if 0 < j < 18:
            ab_ref[18 + j] = got[ROWS:]

    for half in range(2):
        lanes = slice(half * LANES, (half + 1) * LANES)
        prec = jnp.broadcast_to(precisions[half], (8, LANES))

        def scores(i, peak):
            rows = pl.ds(pl.multiple_of(i * 8, 8), 8)
            a = [ab_ref[j, rows, lanes] for j in range(19)]
            b = [None] + [ab_ref[18 + j, rows, lanes] for j in range(1, 18)]
            base = base_ref[rows, lanes]
            correlation = to_rotations(a, b)
            for r in range(ROTATIONS):
                score = correlation[r] * prec + (base + prior_ref[r : r + 1, lanes])
                e_ref[r, rows, lanes] = score
                peak = jnp.maximum(peak, score)
            return peak

        peak = lax.fori_loop(0, ROWS // 8, scores, jnp.full((8, LANES), EXCLUDED, jnp.float32), unroll=True)
        peak = jnp.broadcast_to(jnp.max(peak, axis=0, keepdims=True), (8, LANES))

        def masses(i, mass):
            rows = pl.ds(pl.multiple_of(i * 8, 8), 8)
            for r in range(ROTATIONS):
                e = jnp.exp(e_ref[r, rows, lanes] - peak)
                e_ref[r, rows, lanes] = e
                mass = mass + e
            return mass

        mass = lax.fori_loop(0, ROWS // 8, masses, jnp.zeros((8, LANES), jnp.float32), unroll=True)
        stat_ref[0:8, lanes] = peak
        stat_ref[8:16, lanes] = jnp.broadcast_to(jnp.sum(mass, axis=0, keepdims=True), (8, LANES))


def spectrum_kernel(e_ref, w_ref):
    for half in range(2):
        lanes = slice(half * LANES, (half + 1) * LANES)

        def spectra(i, carry):
            rows = pl.ds(pl.multiple_of(i * 8, 8), 8)
            c, s = from_rotations([e_ref[r, rows, lanes] for r in range(ROTATIONS)])
            for j in range(19):
                w_ref[j, rows, lanes] = c[j]
            for j in range(1, 18):
                w_ref[18 + j, rows, lanes] = s[j]
            return carry

        lax.fori_loop(0, ROWS // 8, spectra, 0, unroll=True)


def class_kernel(cls_ref, cp_ref, norm_ref):
    arrange_classes(cls_ref, cp_ref, norm_ref)


def sums_kernel(w_ref, xp_ref, mine, theirs, out_ref, evidence_ref, pc_ref):
    held = lax.broadcasted_iota(jnp.int32, (1, LANES), 1) < OWN

    def settle(half):
        here = slice(half * LANES, (half + 1) * LANES)
        there = slice((1 - half) * LANES, (2 - half) * LANES)
        peak = jnp.maximum(mine[0:1, here], theirs[0:1, there])
        lift = jnp.exp(mine[0:1, here] - peak)
        mass = mine[8:9, here] * lift + theirs[8:9, there] * jnp.exp(theirs[0:1, there] - peak)
        mass = jnp.where(held, mass, 1.0)
        return jnp.where(held, lift / mass, 0.0), peak + jnp.log(mass)

    scale_a, evidence = settle(0)
    scale_b, _ = settle(1)
    scale = jnp.concatenate([scale_a, scale_b], axis=1)
    evidence_ref[...] = evidence[:, :OWN]

    def weights_of(i):
        return w_ref[i] * scale

    totals = weights_of(0)
    totals = jnp.concatenate([totals, jnp.zeros((LANES - ROWS, COLS), jnp.float32)], axis=0)
    high = totals.astype(jnp.bfloat16)
    low = (totals - high.astype(jnp.float32)).astype(jnp.bfloat16)
    ones = jnp.ones((16, COLS), jnp.bfloat16)
    dims = (((1,), (1,)), ((), ()))
    total = lax.dot_general(ones, high, dims, preferred_element_type=jnp.float32)
    total = total + lax.dot_general(ones, low, dims, preferred_element_type=jnp.float32)
    total = total[0:1]

    for j in range(RESIDUES):
        pair = 0 < j < 18
        weight = weights_of(j)
        if pair:
            weight = jnp.concatenate([weight, weights_of(18 + j)], axis=0)
        else:
            weight = jnp.concatenate([weight, jnp.zeros((8, COLS), jnp.float32)], axis=0)
        high = weight.astype(jnp.bfloat16)
        low = (weight - high.astype(jnp.float32)).astype(jnp.bfloat16)
        lanes = slice(j * COLS, (j + 1) * COLS)
        images = xp_ref[:, lanes]
        dims = (((1,), (0,)), ((), ()))
        got = lax.dot_general(high, images, dims, preferred_element_type=jnp.float32)
        got = got + lax.dot_general(low, images, dims, preferred_element_type=jnp.float32)
        re, im = got[:ROWS, :LANES], got[:ROWS, LANES:]
        if pair:
            sign = sign_lanes(j, ROWS)
            re, im = re - sign * got[ROWS:, LANES:], im + sign * got[ROWS:, :LANES]
        pc_ref[:, j * COLS : j * COLS + LANES] = re * SUM_SCALE
        pc_ref[:, j * COLS + LANES : (j + 1) * COLS] = im * SUM_SCALE

    place = {}
    for j in range(RESIDUES):
        for at, (m, _) in enumerate(MEMBERS[j]):
            place[m] = j * COLS + at * CYCLES
    row = lax.broadcasted_iota(jnp.int32, (HALF_ROWS, LANES), 0)
    for block in range(BLOCKS):
        part, first = divmod(block, BLOCKS // 2)
        starts = [place[first * GROUP + q] + part * LANES for q in range(GROUP)]
        whole = jnp.concatenate([pc_ref[:, at : at + CYCLES] for at in starts], axis=1)
        for half in range(2):
            rows = whole[half * SPLIT : half * SPLIT + HALF_ROWS]
            out_ref[half * BLOCKS + block] = jnp.where(row == TOTAL_ROW, total * SUM_SCALE, rows)


FINISH_STEPS = 4
STEP_BLOCKS = BLOCKS // FINISH_STEPS


def finish_kernel(sum_ref, cls_hbm, out_hbm, cls_ref, out_ref, cls_sem, out_sems):
    fetch = pltpu.make_async_copy(cls_hbm, cls_ref, cls_sem)
    fetch.start()
    row = lax.broadcasted_iota(jnp.int32, (HALF_ROWS, LANES), 0)
    lane = lax.broadcasted_iota(jnp.int32, (HALF_ROWS, LANES), 1)
    share = []
    for half in range(2):
        total = sum_ref[half, 0, TOTAL_ROW : TOTAL_ROW + 1, :]
        weight = jnp.sum(jnp.where(lane == row + half * SPLIT, total, 0.0), axis=1, keepdims=True)
        share.append(1.0 / (weight * (1.0 / SUM_SCALE) + CLASS_PRIOR))
    fetch.wait()
    copies = []
    for step in range(FINISH_STEPS):
        for block in range(step * STEP_BLOCKS, (step + 1) * STEP_BLOCKS):
            lanes = slice(block * LANES, (block + 1) * LANES)
            old = cls_ref[:, lanes].astype(jnp.float32)
            for half in range(2):
                count = SPLIT if half == 0 else CLASSES - SPLIT
                rows = slice(half * SPLIT, half * SPLIT + count)
                new = sum_ref[half, block, 0:count] * (1.0 / SUM_SCALE) + CLASS_PRIOR * old[rows]
                out_ref[rows, lanes] = new * share[half][:count]
        lanes = slice(step * STEP_BLOCKS * LANES, (step + 1) * STEP_BLOCKS * LANES)
        copy = pltpu.make_async_copy(out_ref.at[:, lanes], out_hbm.at[:, lanes], out_sems.at[step])
        copy.start()
        copies.append(copy)
    for copy in copies:
        copy.wait()


VMEM = pl.BlockSpec(memory_space=pltpu.VMEM)
SMEM = pl.BlockSpec(memory_space=pltpu.SMEM)


ANY = pl.BlockSpec(memory_space=pl.ANY)
MIB = 1024 * 1024


def shards(images, precision, rotation_offset, classes, prior_blocks):
    swap = [(0, 1), (1, 0)]
    other_images = lax.ppermute(images, "dom", swap)
    other_precision = lax.ppermute(precision, "dom", swap)
    other_offset = lax.ppermute(rotation_offset, "dom", swap)

    cost = pl.CostEstimate(flops=4 * 10**9, bytes_accessed=8 * MIB, transcendentals=36 * 104 * 128)
    cp, norm = pl.pallas_call(
        class_kernel,
        out_shape=(
            jax.ShapeDtypeStruct((RESIDUES, 2 * ROWS, COLS), jnp.bfloat16),
            jax.ShapeDtypeStruct((ROWS, LANES), jnp.float32),
        ),
        in_specs=[VMEM],
        out_specs=(VMEM,) * 2,
        compiler_params=pltpu.CompilerParams(vmem_limit_bytes=12 * MIB),
        cost_estimate=cost,
        name="classes",
    )(classes)

    e, by_residue, mine = pl.pallas_call(
        score_kernel,
        out_shape=(
            jax.ShapeDtypeStruct((36, ROWS, COLS), jnp.float32),
            jax.ShapeDtypeStruct((COLS, RESIDUES * COLS), jnp.bfloat16),
            jax.ShapeDtypeStruct((16, COLS), jnp.float32),
        ),
        in_specs=[SMEM] + [VMEM] * 8,
        out_specs=(VMEM,) * 3,
        scratch_shapes=[
            pltpu.VMEM((36, ROWS, COLS), jnp.float32),
            pltpu.VMEM((ROWS, COLS), jnp.float32),
            pltpu.VMEM((40, COLS), jnp.float32),
        ],
        compiler_params=pltpu.CompilerParams(vmem_limit_bytes=20 * MIB),
        cost_estimate=cost,
        name="scores",
    )(
        prior_blocks,
        images,
        other_images,
        precision.reshape(1, OWN),
        other_precision.reshape(1, OWN),
        rotation_offset.reshape(1, OWN),
        other_offset.reshape(1, OWN),
        cp,
        norm,
    )
    theirs = lax.ppermute(mine, "dom", swap)

    weights = pl.pallas_call(
        spectrum_kernel,
        out_shape=jax.ShapeDtypeStruct((36, ROWS, COLS), jnp.float32),
        in_specs=[VMEM],
        out_specs=VMEM,
        compiler_params=pltpu.CompilerParams(vmem_limit_bytes=16 * MIB),
        cost_estimate=cost,
        name="spectra",
    )(e)

    parts, evidence = pl.pallas_call(
        sums_kernel,
        out_shape=(
            jax.ShapeDtypeStruct((CHUNKS, HALF_ROWS, LANES), jnp.float32),
            jax.ShapeDtypeStruct((1, OWN), jnp.float32),
        ),
        in_specs=[VMEM] * 4,
        out_specs=(VMEM, VMEM),
        scratch_shapes=[pltpu.VMEM((ROWS, RESIDUES * COLS), jnp.float32)],
        compiler_params=pltpu.CompilerParams(vmem_limit_bytes=20 * MIB),
        name="sums",
    )(weights, by_residue, mine, theirs)

    got = lax.all_to_all(parts.astype(jnp.float16), "cls", 0, 0, tiled=True)
    total = jnp.sum(got.astype(jnp.float32), axis=0).astype(jnp.float16)
    repeated = jnp.broadcast_to(total[None], (CHUNKS, HALF_ROWS, LANES))
    whole = lax.all_to_all(repeated, "cls", 0, 0, tiled=True)
    new_classes = pl.pallas_call(
        finish_kernel,
        out_shape=jax.ShapeDtypeStruct((CLASSES, BLOCKS * LANES), jnp.float32),
        in_specs=[VMEM, ANY],
        out_specs=ANY,
        scratch_shapes=[
            pltpu.VMEM(classes.shape, jnp.bfloat16),
            pltpu.VMEM((CLASSES, BLOCKS * LANES), jnp.float32),
            pltpu.SemaphoreType.DMA,
            pltpu.SemaphoreType.DMA((FINISH_STEPS,)),
        ],
        compiler_params=pltpu.CompilerParams(vmem_limit_bytes=12 * MIB),
        name="finish",
    )(whole.astype(jnp.float32).reshape(2, BLOCKS, HALF_ROWS, LANES), classes)
    return new_classes, evidence.reshape(OWN)


def solution(mesh):
    in_specs = (
        P(("cls", "dom"), None),
        P(("cls", "dom")),
        P(("cls", "dom")),
        P("dom", None),
        P("cls", "dom"),
    )
    out_specs = (P("dom", None), P(("cls", "dom")))
    return jax.shard_map(shards, mesh=mesh, in_specs=in_specs, out_specs=out_specs, check_vma=False)
```

```python
import math

import jax
import jax.numpy as jnp
import numpy as np
from jax import lax
from jax.experimental import pallas as pl
from jax.experimental.pallas import tpu as pltpu
from jax.sharding import PartitionSpec as P

FREQUENCIES = 64
CYCLES = 32
PART = FREQUENCIES * CYCLES
ROTATIONS = 36
CLASS_BLOCK = 5
EXCLUDED = -1e30
PRIOR_WIDTH = 12.0
CLASS_PRIOR = 16.0

RESIDUES = 19
GROUP = 4
LANES = 128
OWN = 96
CLASSES = 100
ROWS = 104
ROWS_16 = 112
SPLIT = 48
HALF_ROWS = 52
QUADS = 13
COLS = 2 * LANES
CHUNKS = 64
BLOCKS = 32
SUM_SCALE = 0.25

MEMBERS = []
for _j in range(RESIDUES):
    _same = [(m, 1) for m in range(FREQUENCIES) if m % ROTATIONS == _j]
    _back = [(m, -1) for m in range(FREQUENCIES) if m % ROTATIONS == (ROTATIONS - _j) % ROTATIONS and _j not in (0, 18)]
    MEMBERS.append(_same + _back)


def cosine(k):
    return float(np.cos(2.0 * np.pi * k / 9.0))


def sine(k):
    return float(np.sin(2.0 * np.pi * k / 9.0))


def nine_cos(x):
    c1, c2 = cosine(1), cosine(2)
    t, u = x[0] + x[3], (x[1] + x[2]) + x[4]
    base = x[0] - 0.5 * x[3]
    p, q = x[1] - x[4], x[2] - x[4]
    y1 = base + (p * c1 + q * c2)
    y2 = base + ((p - q) * c2 - q * c1)
    y4 = base - ((p - q) * c1 + p * c2)
    return [t + u, y1, y2, t - 0.5 * u, y4]


def nine_sin(x):
    s1, s3, s4 = sine(1), sine(3), sine(4)
    p, q = x[1] + x[2], x[2] + x[4]
    d = p - q
    t = x[3] * s3
    return [None, t + (p * s1 + q * s4), (d * s1 + p * s4) - t, ((x[1] - x[2]) + x[4]) * s3, t + (d * s4 - q * s1)]


def fold(j):
    j %= ROTATIONS
    return (j, 1) if j <= 18 else (ROTATIONS - j, -1)


def signed(values, j):
    at, sign = fold(j)
    return values[at] if sign > 0 else -values[at]


def rotation_of(r4, r9):
    return next(r for r in range(ROTATIONS) if r % 4 == r4 and r % 9 == r9)


def to_rotations(a, b):
    one = ([a[0]] + [a[fold(4 * k)[0]] for k in range(1, 5)], [None] + [signed(b, 4 * k) for k in range(1, 5)])
    alt = ([a[18]] + [a[fold(18 + 4 * k)[0]] for k in range(1, 5)], [None] + [signed(b, 18 + 4 * k) for k in range(1, 5)])
    cc, cs, sc, ss = [a[9]], [None], [b[9]], [None]
    for k in range(1, 5):
        a_p, b_p = a[fold(9 + 4 * k)[0]], b[fold(9 + 4 * k)[0]]
        a_m, b_m = a[fold(9 - 4 * k)[0]], b[fold(9 - 4 * k)[0]]
        assert fold(9 + 4 * k)[1] == fold(9 - 4 * k)[1]
        cc.append(a_p + a_m)
        ss.append(a_m - a_p)
        if fold(9 + 4 * k)[1] > 0:
            sc.append(b_p + b_m)
            cs.append(b_p - b_m)
        else:
            sc.append(-(b_p + b_m))
            cs.append(b_m - b_p)
    lines = []
    for even, odd in (one, alt, (cc, cs), (sc, ss)):
        e, o = nine_cos(even), nine_sin(odd)
        lines.append([e[0]] + [e[r] + o[r] for r in range(1, 5)] + [e[9 - r] - o[9 - r] for r in range(5, 9)])
    y = [None] * ROTATIONS
    for r9 in range(9):
        g1, gm, gc, gs = (line[r9] for line in lines)
        plus, minus = g1 + gm, g1 - gm
        y[rotation_of(0, r9)] = plus + gc
        y[rotation_of(2, r9)] = plus - gc
        y[rotation_of(1, r9)] = minus + gs
        y[rotation_of(3, r9)] = minus - gs
    return y


def from_rotations(e):
    lines = [[], [], [], []]
    for r9 in range(9):
        e0, e1, e2, e3 = (e[rotation_of(r4, r9)] for r4 in range(4))
        p, q = e0 + e2, e1 + e3
        for line, value in zip(lines, (p + q, p - q, e0 - e2, e1 - e3)):
            line.append(value)
    spectra = []
    for h in lines:
        even = [h[0]] + [h[k] + h[9 - k] for k in range(1, 5)]
        odd = [None] + [h[k] - h[9 - k] for k in range(1, 5)]
        spectra.append((nine_cos(even), nine_sin(odd)))
    (one_c, one_s), (alt_c, alt_s), (cc, cs), (sc, ss) = spectra
    c, s = [None] * RESIDUES, [None] * RESIDUES
    c[0], c[18], c[9], s[9] = one_c[0], alt_c[0], cc[0], sc[0]
    for k in range(1, 5):
        for first, cosines, sines in ((0, one_c, one_s), (18, alt_c, alt_s)):
            at, sign = fold(first + 4 * k)
            c[at], s[at] = cosines[k], sines[k] if sign > 0 else -sines[k]
        at_p, sign = fold(9 + 4 * k)
        at_m, _ = fold(9 - 4 * k)
        c[at_p], c[at_m] = cc[k] - ss[k], cc[k] + ss[k]
        if sign > 0:
            s[at_p], s[at_m] = sc[k] + cs[k], sc[k] - cs[k]
        else:
            s[at_p], s[at_m] = -(sc[k] + cs[k]), cs[k] - sc[k]
    return c, s


def gather_lanes(ref, part, j):
    rows = ref.shape[0]
    pieces = [ref[:, part * PART + m * CYCLES : part * PART + (m + 1) * CYCLES] for m, _ in MEMBERS[j]]
    if len(pieces) < GROUP:
        pieces.append(jnp.zeros((rows, (GROUP - len(pieces)) * CYCLES), ref.dtype))
    return jnp.concatenate(pieces, axis=1)


def sign_lanes(j, rows):
    lane = lax.broadcasted_iota(jnp.int32, (rows, LANES), 1)
    same = sum(1 for _, s in MEMBERS[j] if s > 0) * CYCLES
    return jnp.where(lane < same, 1.0, -1.0)


def particle_row(values):
    return jnp.concatenate([values, jnp.zeros((1, LANES - OWN), values.dtype)], axis=1)


def score_kernel(blocks_ref, own_ref, other_ref, prec_a, prec_b, offset_a, offset_b, cp_ref, norm_ref, e_ref, xp_ref, stat_ref, top_ref, ab_ref, base_ref, prior_ref):
    row = lax.broadcasted_iota(jnp.int32, (ROWS, LANES), 0)
    dom = lax.axis_index("dom")
    precisions = [particle_row(p[...].astype(jnp.float32)) for p in (prec_a, prec_b)]
    for half in range(2):
        lanes = slice(half * LANES, (half + 1) * LANES)
        block_row = dom if half == 0 else 1 - dom
        admit = jnp.zeros((ROWS, LANES), jnp.int32)
        for block in range(CLASSES // CLASS_BLOCK):
            inside = (row >= block * CLASS_BLOCK) & (row < (block + 1) * CLASS_BLOCK)
            admit = jnp.where(inside, blocks_ref[block_row, block], admit)
        base_ref[:, lanes] = jnp.where(admit == 1, -0.5 * norm_ref[...] * precisions[half], EXCLUDED)
        offset = particle_row((offset_a, offset_b)[half][...])
        steps = lax.rem(lax.broadcasted_iota(jnp.int32, (40, LANES), 0) - offset + ROTATIONS, ROTATIONS)
        distance = jnp.minimum(steps, ROTATIONS - steps).astype(jnp.float32) * (1.0 / PRIOR_WIDTH)
        prior_ref[:, lanes] = -0.5 * distance * distance
    zeros = jnp.zeros((LANES - OWN, RESIDUES * COLS), jnp.bfloat16)
    xp_ref[OWN:LANES] = zeros
    xp_ref[LANES + OWN :] = zeros
    for j in range(RESIDUES):
        for part in range(2):
            at = j * COLS + part * LANES
            xp_ref[0:OWN, at : at + LANES] = gather_lanes(own_ref, part, j)
            xp_ref[LANES : LANES + OWN, at : at + LANES] = gather_lanes(other_ref, part, j)
        pair = 0 < j < 18
        operand = cp_ref[j] if pair else cp_ref[j, :ROWS_16]
        got = lax.dot_general(
            operand, xp_ref[:, j * COLS : (j + 1) * COLS], (((1,), (1,)), ((), ())), preferred_element_type=jnp.float32
        )
        ab_ref[j] = got[:ROWS]
        if pair:
            ab_ref[18 + j] = got[ROWS_16 : ROWS_16 + ROWS]

    for half in range(2):
        lanes = slice(half * LANES, (half + 1) * LANES)
        prec = jnp.broadcast_to(precisions[half], (8, LANES))

        def scores(i, carry):
            peak, mass = carry
            rows = pl.ds(pl.multiple_of(i * 8, 8), 8)
            a = [ab_ref[j, rows, lanes] for j in range(19)]
            b = [None] + [ab_ref[18 + j, rows, lanes] for j in range(1, 18)]
            base = base_ref[rows, lanes]
            correlation = to_rotations(a, b)
            score = [correlation[r] * prec + (base + prior_ref[r : r + 1, lanes]) for r in range(ROTATIONS)]
            top = score[0]
            for r in range(1, ROTATIONS):
                top = jnp.maximum(top, score[r])
            total = None
            for r in range(ROTATIONS):
                e = jnp.exp(score[r] - top)
                e_ref[r, rows, lanes] = e
                total = e if total is None else total + e
            top_ref[rows, lanes] = top
            higher = jnp.maximum(peak, top)
            mass = mass * jnp.exp(peak - higher) + total * jnp.exp(top - higher)
            return higher, mass

        start = (jnp.full((8, LANES), EXCLUDED, jnp.float32), jnp.zeros((8, LANES), jnp.float32))
        tops, mass = lax.fori_loop(0, ROWS // 8, scores, start, unroll=True)
        peak = jnp.max(tops, axis=0, keepdims=True)
        mass = jnp.sum(mass * jnp.exp(tops - peak), axis=0, keepdims=True)
        stat_ref[0:8, lanes] = jnp.broadcast_to(peak, (8, LANES))
        stat_ref[8:16, lanes] = jnp.broadcast_to(mass, (8, LANES))


def spectrum_kernel(e_ref, top_ref, stat_ref, w_ref):
    for half in range(2):
        lanes = slice(half * LANES, (half + 1) * LANES)

        peak = stat_ref[0:8, lanes]

        def spectra(i, carry):
            rows = pl.ds(pl.multiple_of(i * 8, 8), 8)
            lift = jnp.exp(top_ref[rows, lanes] - peak)
            c, s = from_rotations([e_ref[r, rows, lanes] * lift for r in range(ROTATIONS)])
            for j in range(19):
                w_ref[j, rows, lanes] = c[j]
            for j in range(1, 18):
                w_ref[18 + j, rows, lanes] = s[j]
            return carry

        lax.fori_loop(0, ROWS // 8, spectra, 0, unroll=True)


def class_kernel(cls_ref, cp_ref, norm_ref):
    pad = jnp.zeros((ROWS_16 - CLASSES, LANES), jnp.bfloat16)
    for j in range(RESIDUES):
        c_re = jnp.concatenate([gather_lanes(cls_ref, 0, j), pad], axis=0)
        c_im = jnp.concatenate([gather_lanes(cls_ref, 1, j), pad], axis=0)
        cp_ref[j, :ROWS_16, :LANES] = c_re
        cp_ref[j, :ROWS_16, LANES:] = c_im
        if 0 < j < 18:
            sign = sign_lanes(j, ROWS_16).astype(jnp.bfloat16)
            cp_ref[j, ROWS_16:, :LANES] = c_im * sign
            cp_ref[j, ROWS_16:, LANES:] = -(c_re * sign)
    norm = jnp.zeros((CLASSES, LANES), jnp.float32)
    for block in range(BLOCKS):
        member = cls_ref[:, block * LANES : (block + 1) * LANES].astype(jnp.float32)
        norm = norm + member * member
    norm = jnp.broadcast_to(jnp.sum(norm, axis=1, keepdims=True), (CLASSES, LANES))
    norm_ref[...] = jnp.concatenate([norm, jnp.zeros((ROWS - CLASSES, LANES), jnp.float32)], axis=0)


def sums_kernel(w_ref, xp_ref, mine, theirs, out_ref, evidence_ref, pc_ref):
    held = lax.broadcasted_iota(jnp.int32, (1, LANES), 1) < OWN

    def settle(half):
        here = slice(half * LANES, (half + 1) * LANES)
        there = slice((1 - half) * LANES, (2 - half) * LANES)
        peak = jnp.maximum(mine[0:1, here], theirs[0:1, there])
        lift = jnp.exp(mine[0:1, here] - peak)
        mass = mine[8:9, here] * lift + theirs[8:9, there] * jnp.exp(theirs[0:1, there] - peak)
        mass = jnp.where(held, mass, 1.0)
        return jnp.where(held, lift / mass, 0.0), peak + jnp.log(mass)

    scale_a, evidence = settle(0)
    scale_b, _ = settle(1)
    scale = jnp.concatenate([scale_a, scale_b], axis=1)
    evidence_ref[...] = evidence[:, :OWN]

    def weights_of(i):
        return w_ref[i] * scale

    totals = weights_of(0)
    totals = jnp.concatenate([totals, jnp.zeros((LANES - ROWS, COLS), jnp.float32)], axis=0)
    high = totals.astype(jnp.bfloat16)
    low = (totals - high.astype(jnp.float32)).astype(jnp.bfloat16)
    ones = jnp.ones((16, COLS), jnp.bfloat16)
    dims = (((1,), (1,)), ((), ()))
    total = lax.dot_general(ones, high, dims, preferred_element_type=jnp.float32)
    total = total + lax.dot_general(ones, low, dims, preferred_element_type=jnp.float32)
    total = total[0:1]

    for j in range(RESIDUES):
        pair = 0 < j < 18
        weight = weights_of(j)
        if pair:
            weight = jnp.concatenate([weight, weights_of(18 + j)], axis=0)
        else:
            weight = jnp.concatenate([weight, jnp.zeros((8, COLS), jnp.float32)], axis=0)
        high = weight.astype(jnp.bfloat16)
        low = (weight - high.astype(jnp.float32)).astype(jnp.bfloat16)
        lanes = slice(j * COLS, (j + 1) * COLS)
        images = xp_ref[:, lanes]
        dims = (((1,), (0,)), ((), ()))
        got = lax.dot_general(high, images, dims, preferred_element_type=jnp.float32)
        got = got + lax.dot_general(low, images, dims, preferred_element_type=jnp.float32)
        re, im = got[:ROWS, :LANES], got[:ROWS, LANES:]
        if pair:
            sign = sign_lanes(j, ROWS)
            re, im = re - sign * got[ROWS:, LANES:], im + sign * got[ROWS:, :LANES]
        pc_ref[:, j * COLS : j * COLS + LANES] = re * SUM_SCALE
        pc_ref[:, j * COLS + LANES : (j + 1) * COLS] = im * SUM_SCALE

    place = {}
    for j in range(RESIDUES):
        for at, (m, _) in enumerate(MEMBERS[j]):
            place[m] = j * COLS + at * CYCLES
    row = lax.broadcasted_iota(jnp.int32, (HALF_ROWS, LANES), 0)
    for block in range(BLOCKS):
        part, first = divmod(block, BLOCKS // 2)
        starts = [place[first * GROUP + q] + part * LANES for q in range(GROUP)]
        whole = jnp.concatenate([pc_ref[:, at : at + CYCLES] for at in starts], axis=1)
        for half in range(2):
            rows = whole[half * SPLIT : half * SPLIT + HALF_ROWS]
            if half == 0:
                rows = jnp.where(row == SPLIT, total * SUM_SCALE, rows)
            out_ref[half * BLOCKS + block] = rows.reshape(QUADS, 4, LANES)


FINISH_STEPS = 4
STEP_BLOCKS = BLOCKS // FINISH_STEPS


def finish_kernel(sum_ref, cls_hbm, out_hbm, cls_ref, out_ref, cls_sem, out_sems):
    fetch = pltpu.make_async_copy(cls_hbm, cls_ref, cls_sem)
    fetch.start()
    row = lax.broadcasted_iota(jnp.int32, (HALF_ROWS, LANES), 0)
    lane = lax.broadcasted_iota(jnp.int32, (HALF_ROWS, LANES), 1)
    share = []
    total = sum_ref[0, 0, SPLIT // 4, 0:1, :]
    for half in range(2):
        weight = jnp.sum(jnp.where(lane == row + half * SPLIT, total, 0.0), axis=1, keepdims=True)
        share.append(1.0 / (weight * (1.0 / SUM_SCALE) + CLASS_PRIOR))
    fetch.wait()
    copies = []
    for step in range(FINISH_STEPS):
        for block in range(step * STEP_BLOCKS, (step + 1) * STEP_BLOCKS):
            lanes = slice(block * LANES, (block + 1) * LANES)
            old = cls_ref[:, lanes].astype(jnp.float32)
            for half in range(2):
                count = SPLIT if half == 0 else CLASSES - SPLIT
                rows = slice(half * SPLIT, half * SPLIT + count)
                new = sum_ref[half, block].reshape(HALF_ROWS, LANES)[:count] * (1.0 / SUM_SCALE) + CLASS_PRIOR * old[rows]
                out_ref[rows, lanes] = new * share[half][:count]
        lanes = slice(step * STEP_BLOCKS * LANES, (step + 1) * STEP_BLOCKS * LANES)
        copy = pltpu.make_async_copy(out_ref.at[:, lanes], out_hbm.at[:, lanes], out_sems.at[step])
        copy.start()
        copies.append(copy)
    for copy in copies:
        copy.wait()


VMEM = pl.BlockSpec(memory_space=pltpu.VMEM)
SMEM = pl.BlockSpec(memory_space=pltpu.SMEM)


ANY = pl.BlockSpec(memory_space=pl.ANY)
MIB = 1024 * 1024


def shards(images, precision, rotation_offset, classes, prior_blocks):
    swap = [(0, 1), (1, 0)]
    other_images = lax.ppermute(images, "dom", swap)
    other_precision = lax.ppermute(precision, "dom", swap)
    other_offset = lax.ppermute(rotation_offset, "dom", swap)

    cost = pl.CostEstimate(flops=4 * 10**9, bytes_accessed=8 * MIB, transcendentals=36 * 104 * 128)
    cp, norm = pl.pallas_call(
        class_kernel,
        out_shape=(
            jax.ShapeDtypeStruct((RESIDUES, 2 * ROWS_16, COLS), jnp.bfloat16),
            jax.ShapeDtypeStruct((ROWS, LANES), jnp.float32),
        ),
        in_specs=[VMEM],
        out_specs=(VMEM,) * 2,
        compiler_params=pltpu.CompilerParams(vmem_limit_bytes=12 * MIB),
        cost_estimate=cost,
        name="classes",
    )(classes)

    e, by_residue, mine, tops = pl.pallas_call(
        score_kernel,
        out_shape=(
            jax.ShapeDtypeStruct((36, ROWS, COLS), jnp.float32),
            jax.ShapeDtypeStruct((COLS, RESIDUES * COLS), jnp.bfloat16),
            jax.ShapeDtypeStruct((16, COLS), jnp.float32),
            jax.ShapeDtypeStruct((ROWS, COLS), jnp.float32),
        ),
        in_specs=[SMEM] + [VMEM] * 8,
        out_specs=(VMEM,) * 4,
        scratch_shapes=[
            pltpu.VMEM((36, ROWS, COLS), jnp.float32),
            pltpu.VMEM((ROWS, COLS), jnp.float32),
            pltpu.VMEM((40, COLS), jnp.float32),
        ],
        compiler_params=pltpu.CompilerParams(vmem_limit_bytes=20 * MIB),
        cost_estimate=cost,
        name="scores",
    )(
        prior_blocks,
        images,
        other_images,
        precision.reshape(1, OWN),
        other_precision.reshape(1, OWN),
        rotation_offset.reshape(1, OWN),
        other_offset.reshape(1, OWN),
        cp,
        norm,
    )
    theirs = lax.ppermute(mine, "dom", swap)

    weights = pl.pallas_call(
        spectrum_kernel,
        out_shape=jax.ShapeDtypeStruct((36, ROWS, COLS), jnp.float32),
        in_specs=[VMEM] * 3,
        out_specs=VMEM,
        compiler_params=pltpu.CompilerParams(vmem_limit_bytes=16 * MIB),
        cost_estimate=cost,
        name="spectra",
    )(e, tops, mine)

    parts, evidence = pl.pallas_call(
        sums_kernel,
        out_shape=(
            jax.ShapeDtypeStruct((CHUNKS, QUADS, 4, LANES), jnp.float32),
            jax.ShapeDtypeStruct((1, OWN), jnp.float32),
        ),
        in_specs=[VMEM] * 4,
        out_specs=(VMEM, VMEM),
        scratch_shapes=[pltpu.VMEM((ROWS, RESIDUES * COLS), jnp.float32)],
        compiler_params=pltpu.CompilerParams(vmem_limit_bytes=20 * MIB),
        name="sums",
    )(weights, by_residue, mine, theirs)

    got = lax.all_to_all(parts.astype(jnp.float16), "cls", 0, 0, tiled=True)
    total = jnp.sum(got.astype(jnp.float32), axis=0).astype(jnp.float16)
    repeated = jnp.broadcast_to(total[None], (CHUNKS, QUADS, 4, LANES))
    whole = lax.all_to_all(repeated, "cls", 0, 0, tiled=True)
    new_classes = pl.pallas_call(
        finish_kernel,
        out_shape=jax.ShapeDtypeStruct((CLASSES, BLOCKS * LANES), jnp.float32),
        in_specs=[VMEM, ANY],
        out_specs=ANY,
        scratch_shapes=[
            pltpu.VMEM(classes.shape, jnp.bfloat16),
            pltpu.VMEM((CLASSES, BLOCKS * LANES), jnp.float32),
            pltpu.SemaphoreType.DMA,
            pltpu.SemaphoreType.DMA((FINISH_STEPS,)),
        ],
        compiler_params=pltpu.CompilerParams(vmem_limit_bytes=12 * MIB),
        name="finish",
    )(whole.astype(jnp.float32).reshape(2, BLOCKS, QUADS, 4, LANES), classes)
    return new_classes, evidence.reshape(OWN)


def solution(mesh):
    in_specs = (
        P(("cls", "dom"), None),
        P(("cls", "dom")),
        P(("cls", "dom")),
        P("dom", None),
        P("cls", "dom"),
    )
    out_specs = (P("dom", None), P(("cls", "dom")))
    return jax.shard_map(shards, mesh=mesh, in_specs=in_specs, out_specs=out_specs, check_vma=False)
```

```python
import math

import jax
import jax.numpy as jnp
import numpy as np
from jax import lax
from jax.experimental import pallas as pl
from jax.experimental.pallas import tpu as pltpu
from jax.sharding import PartitionSpec as P

FREQUENCIES = 64
CYCLES = 32
PART = FREQUENCIES * CYCLES
ROTATIONS = 36
CLASS_BLOCK = 5
EXCLUDED = -1e30
PRIOR_WIDTH = 12.0
CLASS_PRIOR = 16.0

RESIDUES = 19
GROUP = 4
LANES = 128
OWN = 96
CLASSES = 100
ROWS = 104
ROWS_16 = 112
SPLIT = 48
HALF_ROWS = 52
QUADS = 13
COLS = 2 * LANES
CHUNKS = 64
BLOCKS = 32
SUM_SCALE = 0.25

SLOTS = [
    (0, 3), (1, 0, 3), (2, 1, 0), (3, 2, 1), (1, 3, 0), (1, 0, 3), (3, 1, 2), (0, 3, 1), (1, 3, 0), (2, 1, 0, 3),
    (3, 1, 0, 2), (0, 3, 2, 1), (3, 1, 2, 0), (0, 1, 2, 3), (1, 3, 2, 0), (2, 3, 0, 1), (1, 0, 3, 2), (2, 1, 0, 3), (3, 2),
]
PLACE = {}
for _j in range(RESIDUES):
    _same = [(m, 1) for m in range(FREQUENCIES) if m % ROTATIONS == _j]
    _back = [(m, -1) for m in range(FREQUENCIES) if m % ROTATIONS == (ROTATIONS - _j) % ROTATIONS and _j not in (0, 18)]
    for (_m, _sign), _slot in zip(_same + _back, SLOTS[_j], strict=True):
        PLACE[_m] = (_j, _slot, _sign)


def quarter_of(rows):
    return lax.broadcasted_iota(jnp.int32, (rows, LANES), 1) // CYCLES


class Rotated:
    def __init__(self, tile):
        self.tile, self.done = tile, {}

    def __call__(self, at, quarters):
        key = (at, quarters % GROUP)
        if key not in self.done:
            value = self(at, 0) if key[1] else self.tile(at)
            self.done[key] = pltpu.roll(value, key[1] * CYCLES, 1) if key[1] else value
        return self.done[key]


def by_quarter(pieces, quarter):
    whole = None
    for at, piece in pieces.items():
        if whole is None:
            whole = piece if len(pieces) == GROUP else jnp.where(quarter == at, piece, jnp.zeros_like(piece))
        else:
            whole = jnp.where(quarter == at, piece, whole)
    return whole


def to_residues(tile, rows):
    quarter = quarter_of(rows)
    rotated = Rotated(tile)
    for j in range(RESIDUES):
        pieces = {q: rotated(m // GROUP, q - m) for m, (i, q, _) in PLACE.items() if i == j}
        yield j, by_quarter(pieces, quarter)


def cosine(k):
    return float(np.cos(2.0 * np.pi * k / 9.0))


def sine(k):
    return float(np.sin(2.0 * np.pi * k / 9.0))


def nine_cos(x):
    c1, c2 = cosine(1), cosine(2)
    t, u = x[0] + x[3], (x[1] + x[2]) + x[4]
    base = x[0] - 0.5 * x[3]
    p, q = x[1] - x[4], x[2] - x[4]
    y1 = base + (p * c1 + q * c2)
    y2 = base + ((p - q) * c2 - q * c1)
    y4 = base - ((p - q) * c1 + p * c2)
    return [t + u, y1, y2, t - 0.5 * u, y4]


def nine_sin(x):
    s1, s3, s4 = sine(1), sine(3), sine(4)
    p, q = x[1] + x[2], x[2] + x[4]
    d = p - q
    t = x[3] * s3
    return [None, t + (p * s1 + q * s4), (d * s1 + p * s4) - t, ((x[1] - x[2]) + x[4]) * s3, t + (d * s4 - q * s1)]


def fold(j):
    j %= ROTATIONS
    return (j, 1) if j <= 18 else (ROTATIONS - j, -1)


def signed(values, j):
    at, sign = fold(j)
    return values[at] if sign > 0 else -values[at]


def rotation_of(r4, r9):
    return next(r for r in range(ROTATIONS) if r % 4 == r4 and r % 9 == r9)


def to_rotations(a, b):
    one = ([a[0]] + [a[fold(4 * k)[0]] for k in range(1, 5)], [None] + [signed(b, 4 * k) for k in range(1, 5)])
    alt = ([a[18]] + [a[fold(18 + 4 * k)[0]] for k in range(1, 5)], [None] + [signed(b, 18 + 4 * k) for k in range(1, 5)])
    cc, cs, sc, ss = [a[9]], [None], [b[9]], [None]
    for k in range(1, 5):
        a_p, b_p = a[fold(9 + 4 * k)[0]], b[fold(9 + 4 * k)[0]]
        a_m, b_m = a[fold(9 - 4 * k)[0]], b[fold(9 - 4 * k)[0]]
        assert fold(9 + 4 * k)[1] == fold(9 - 4 * k)[1]
        cc.append(a_p + a_m)
        ss.append(a_m - a_p)
        if fold(9 + 4 * k)[1] > 0:
            sc.append(b_p + b_m)
            cs.append(b_p - b_m)
        else:
            sc.append(-(b_p + b_m))
            cs.append(b_m - b_p)
    lines = []
    for even, odd in (one, alt, (cc, cs), (sc, ss)):
        e, o = nine_cos(even), nine_sin(odd)
        lines.append([e[0]] + [e[r] + o[r] for r in range(1, 5)] + [e[9 - r] - o[9 - r] for r in range(5, 9)])
    y = [None] * ROTATIONS
    for r9 in range(9):
        g1, gm, gc, gs = (line[r9] for line in lines)
        plus, minus = g1 + gm, g1 - gm
        y[rotation_of(0, r9)] = plus + gc
        y[rotation_of(2, r9)] = plus - gc
        y[rotation_of(1, r9)] = minus + gs
        y[rotation_of(3, r9)] = minus - gs
    return y


def from_rotations(e):
    lines = [[], [], [], []]
    for r9 in range(9):
        e0, e1, e2, e3 = (e[rotation_of(r4, r9)] for r4 in range(4))
        p, q = e0 + e2, e1 + e3
        for line, value in zip(lines, (p + q, p - q, e0 - e2, e1 - e3)):
            line.append(value)
    spectra = []
    for h in lines:
        even = [h[0]] + [h[k] + h[9 - k] for k in range(1, 5)]
        odd = [None] + [h[k] - h[9 - k] for k in range(1, 5)]
        spectra.append((nine_cos(even), nine_sin(odd)))
    (one_c, one_s), (alt_c, alt_s), (cc, cs), (sc, ss) = spectra
    c, s = [None] * RESIDUES, [None] * RESIDUES
    c[0], c[18], c[9], s[9] = one_c[0], alt_c[0], cc[0], sc[0]
    for k in range(1, 5):
        for first, cosines, sines in ((0, one_c, one_s), (18, alt_c, alt_s)):
            at, sign = fold(first + 4 * k)
            c[at], s[at] = cosines[k], sines[k] if sign > 0 else -sines[k]
        at_p, sign = fold(9 + 4 * k)
        at_m, _ = fold(9 - 4 * k)
        c[at_p], c[at_m] = cc[k] - ss[k], cc[k] + ss[k]
        if sign > 0:
            s[at_p], s[at_m] = sc[k] + cs[k], sc[k] - cs[k]
        else:
            s[at_p], s[at_m] = -(sc[k] + cs[k]), cs[k] - sc[k]
    return c, s


def sign_lanes(j, rows):
    quarter = quarter_of(rows)
    sign = jnp.ones((rows, LANES), jnp.float32)
    for i, q, direction in PLACE.values():
        if i == j and direction < 0:
            sign = jnp.where(quarter == q, -1.0, sign)
    return sign


def particle_row(values):
    return jnp.concatenate([values, jnp.zeros((1, LANES - OWN), values.dtype)], axis=1)


def score_kernel(blocks_ref, own_ref, other_ref, prec_a, prec_b, offset_a, offset_b, cp_ref, norm_ref, e_ref, xp_ref, stat_ref, top_ref, ab_ref, base_ref, prior_ref):
    blocks = CLASSES // CLASS_BLOCK
    first = lax.broadcasted_iota(jnp.int32, (ROWS, blocks), 1) * CLASS_BLOCK
    row = lax.broadcasted_iota(jnp.int32, (ROWS, blocks), 0)
    inside = (row >= first) & (row < first + CLASS_BLOCK)
    swapped = lax.axis_index("dom") == 1
    allowed = [blocks_ref[0:1], blocks_ref[1:2]]
    precisions = [particle_row(p[...].astype(jnp.float32)) for p in (prec_a, prec_b)]
    for half in range(2):
        lanes = slice(half * LANES, (half + 1) * LANES)
        admit = jnp.where(swapped, allowed[1 - half], allowed[half]) == 1
        admit = jnp.sum(jnp.where(inside & admit, 1.0, 0.0), axis=1, keepdims=True)
        base_ref[:, lanes] = jnp.where(admit > 0.0, -0.5 * norm_ref[...] * precisions[half], EXCLUDED)
        offset = particle_row((offset_a, offset_b)[half][...])
        steps = lax.rem(lax.broadcasted_iota(jnp.int32, (40, LANES), 0) - offset + ROTATIONS, ROTATIONS)
        distance = jnp.minimum(steps, ROTATIONS - steps).astype(jnp.float32) * (1.0 / PRIOR_WIDTH)
        prior_ref[:, lanes] = -0.5 * distance * distance
    zeros = jnp.zeros((LANES - OWN, RESIDUES * COLS), jnp.bfloat16)
    xp_ref[OWN:LANES] = zeros
    xp_ref[LANES + OWN :] = zeros
    for first_row, ref in ((0, own_ref), (LANES, other_ref)):
        for part in range(2):
            for i in range(0, OWN, 16):
                tiles = lambda t: ref[i : i + 16, part * PART + t * LANES : part * PART + (t + 1) * LANES]
                for j, value in to_residues(tiles, 16):
                    at = j * COLS + part * LANES
                    xp_ref[first_row + i : first_row + i + 16, at : at + LANES] = value
    for j in range(RESIDUES):
        pair = 0 < j < 18
        operand = cp_ref[j] if pair else cp_ref[j, :ROWS_16]
        got = lax.dot_general(
            operand, xp_ref[:, j * COLS : (j + 1) * COLS], (((1,), (1,)), ((), ())), preferred_element_type=jnp.float32
        )
        ab_ref[j] = got[:ROWS]
        if pair:
            ab_ref[18 + j] = got[ROWS_16 : ROWS_16 + ROWS]

    for half in range(2):
        lanes = slice(half * LANES, (half + 1) * LANES)
        prec = jnp.broadcast_to(precisions[half], (8, LANES))

        def scores(i, carry):
            peak, mass = carry
            rows = pl.ds(pl.multiple_of(i * 8, 8), 8)
            a = [ab_ref[j, rows, lanes] for j in range(19)]
            b = [None] + [ab_ref[18 + j, rows, lanes] for j in range(1, 18)]
            base = base_ref[rows, lanes]
            correlation = to_rotations(a, b)
            score = [correlation[r] * prec + (base + prior_ref[r : r + 1, lanes]) for r in range(ROTATIONS)]
            top = score[0]
            for r in range(1, ROTATIONS):
                top = jnp.maximum(top, score[r])
            total = None
            for r in range(ROTATIONS):
                e = jnp.exp(score[r] - top)
                e_ref[r, rows, lanes] = e
                total = e if total is None else total + e
            top_ref[rows, lanes] = top
            higher = jnp.maximum(peak, top)
            mass = mass * jnp.exp(peak - higher) + total * jnp.exp(top - higher)
            return higher, mass

        start = (jnp.full((8, LANES), EXCLUDED, jnp.float32), jnp.zeros((8, LANES), jnp.float32))
        tops, mass = lax.fori_loop(0, ROWS // 8, scores, start, unroll=True)
        peak = jnp.max(tops, axis=0, keepdims=True)
        mass = jnp.sum(mass * jnp.exp(tops - peak), axis=0, keepdims=True)
        stat_ref[0:8, lanes] = jnp.broadcast_to(peak, (8, LANES))
        stat_ref[8:16, lanes] = jnp.broadcast_to(mass, (8, LANES))


def spectrum_kernel(e_ref, top_ref, stat_ref, w_ref):
    for half in range(2):
        lanes = slice(half * LANES, (half + 1) * LANES)

        peak = stat_ref[0:8, lanes]

        def spectra(i, carry):
            rows = pl.ds(pl.multiple_of(i * 8, 8), 8)
            lift = jnp.exp(top_ref[rows, lanes] - peak)
            c, s = from_rotations([e_ref[r, rows, lanes] * lift for r in range(ROTATIONS)])
            for j in range(19):
                w_ref[j, rows, lanes] = c[j]
            for j in range(1, 18):
                w_ref[18 + j, rows, lanes] = s[j]
            return carry

        lax.fori_loop(0, ROWS // 8, spectra, 0, unroll=True)


def class_kernel(cls_ref, cp_ref, norm_ref):
    pad = jnp.zeros((ROWS_16 - CLASSES, LANES), jnp.bfloat16)
    for part in range(2):
        tiles = lambda t: cls_ref[:, part * PART + t * LANES : part * PART + (t + 1) * LANES]
        for j, value in to_residues(tiles, CLASSES):
            value = jnp.concatenate([value, pad], axis=0)
            cp_ref[j, :ROWS_16, part * LANES : (part + 1) * LANES] = value
            if 0 < j < 18:
                sign = sign_lanes(j, ROWS_16) * (1.0 if part else -1.0)
                cp_ref[j, ROWS_16:, (1 - part) * LANES : (2 - part) * LANES] = value * sign.astype(jnp.bfloat16)
    norm = jnp.zeros((CLASSES, LANES), jnp.float32)
    for block in range(BLOCKS):
        member = cls_ref[:, block * LANES : (block + 1) * LANES].astype(jnp.float32)
        norm = norm + member * member
    norm = jnp.broadcast_to(jnp.sum(norm, axis=1, keepdims=True), (CLASSES, LANES))
    norm_ref[...] = jnp.concatenate([norm, jnp.zeros((ROWS - CLASSES, LANES), jnp.float32)], axis=0)


def settle(mine, theirs, half):
    here = slice(half * LANES, (half + 1) * LANES)
    there = slice((1 - half) * LANES, (2 - half) * LANES)
    peak = jnp.maximum(mine[0:1, here], theirs[0:1, there])
    mass = mine[8:9, here] * jnp.exp(mine[0:1, here] - peak)
    mass = mass + theirs[8:9, there] * jnp.exp(theirs[0:1, there] - peak)
    held = lax.broadcasted_iota(jnp.int32, (1, LANES), 1) < OWN
    return held, peak, jnp.where(held, mass, 1.0)


def sums_kernel(w_ref, xp_ref, mine, theirs, out_ref, pc_ref):
    scale = []
    for half in range(2):
        held, peak, mass = settle(mine, theirs, half)
        lift = jnp.exp(mine[0:1, half * LANES : (half + 1) * LANES] - peak)
        scale.append(jnp.where(held, lift * SUM_SCALE / mass, 0.0))
    scale = jnp.concatenate(scale, axis=1)

    def weights_of(i):
        return w_ref[i] * scale

    totals = weights_of(0)
    totals = jnp.concatenate([totals, jnp.zeros((LANES - ROWS, COLS), jnp.float32)], axis=0)
    high = totals.astype(jnp.bfloat16)
    low = (totals - high.astype(jnp.float32)).astype(jnp.bfloat16)
    ones = jnp.ones((16, COLS), jnp.bfloat16)
    dims = (((1,), (1,)), ((), ()))
    total = lax.dot_general(ones, high, dims, preferred_element_type=jnp.float32)
    total = total + lax.dot_general(ones, low, dims, preferred_element_type=jnp.float32)
    total = total[0:1]

    for j in range(RESIDUES):
        pair = 0 < j < 18
        weight = weights_of(j)
        if pair:
            weight = jnp.concatenate([weight, weights_of(18 + j)], axis=0)
        else:
            weight = jnp.concatenate([weight, jnp.zeros((8, COLS), jnp.float32)], axis=0)
        high = weight.astype(jnp.bfloat16)
        low = (weight - high.astype(jnp.float32)).astype(jnp.bfloat16)
        lanes = slice(j * COLS, (j + 1) * COLS)
        images = xp_ref[:, lanes]
        dims = (((1,), (0,)), ((), ()))
        got = lax.dot_general(high, images, dims, preferred_element_type=jnp.float32)
        got = got + lax.dot_general(low, images, dims, preferred_element_type=jnp.float32)
        re, im = got[:ROWS, :LANES], got[:ROWS, LANES:]
        if pair:
            sign = sign_lanes(j, ROWS)
            re, im = re - sign * got[ROWS:, LANES:], im + sign * got[ROWS:, :LANES]
        pc_ref[:, j * COLS : j * COLS + LANES] = re
        pc_ref[:, j * COLS + LANES : (j + 1) * COLS] = im

    quarter = quarter_of(8)
    last = jnp.broadcast_to(total, (4, LANES))
    for part in range(2):
        for i in range(ROWS // 8):
            rotated = Rotated(lambda j: pc_ref[i * 8 : (i + 1) * 8, j * COLS + part * LANES : j * COLS + (part + 1) * LANES])
            for t in range(BLOCKS // 2):
                pieces = {m % GROUP: rotated(PLACE[m][0], m - PLACE[m][1]) for m in range(t * GROUP, (t + 1) * GROUP)}
                value = by_quarter(pieces, quarter)
                half, at = divmod(i, SPLIT // 8) if i < ROWS // 8 - 1 else (1, i - SPLIT // 8)
                block = half * BLOCKS + part * (BLOCKS // 2) + t
                if i == ROWS // 8 - 1:
                    out_ref[block, QUADS - 1] = value[:4]
                else:
                    out_ref[block, 2 * at : 2 * at + 2] = value.reshape(2, 4, LANES)
                if half == 0 and at == 0:
                    out_ref[block, QUADS - 1] = last


FINISH_STEPS = 4
STEP_BLOCKS = BLOCKS // FINISH_STEPS


def finish_kernel(sum_ref, cls_ref, mine, theirs, out_hbm, evidence_hbm, out_ref, evidence_ref, out_sems, evidence_sem):
    _, peak, mass = settle(mine, theirs, 0)
    evidence_ref[...] = (peak + jnp.log(mass))[:, :OWN]
    send = pltpu.make_async_copy(evidence_ref, evidence_hbm, evidence_sem)
    send.start()
    row = lax.broadcasted_iota(jnp.int32, (HALF_ROWS, LANES), 0)
    lane = lax.broadcasted_iota(jnp.int32, (HALF_ROWS, LANES), 1)
    share = []
    total = sum_ref[0, 0, SPLIT // 4, 0:1, :]
    for half in range(2):
        weight = jnp.sum(jnp.where(lane == row + half * SPLIT, total, 0.0), axis=1, keepdims=True)
        share.append(1.0 / (weight * (1.0 / SUM_SCALE) + CLASS_PRIOR))
    copies = []
    for step in range(FINISH_STEPS):
        for block in range(step * STEP_BLOCKS, (step + 1) * STEP_BLOCKS):
            lanes = slice(block * LANES, (block + 1) * LANES)
            old = cls_ref[:, lanes].astype(jnp.float32)
            for half in range(2):
                count = SPLIT if half == 0 else CLASSES - SPLIT
                rows = slice(half * SPLIT, half * SPLIT + count)
                new = sum_ref[half, block].reshape(HALF_ROWS, LANES)[:count] * (1.0 / SUM_SCALE) + CLASS_PRIOR * old[rows]
                out_ref[rows, lanes] = new * share[half][:count]
        lanes = slice(step * STEP_BLOCKS * LANES, (step + 1) * STEP_BLOCKS * LANES)
        copy = pltpu.make_async_copy(out_ref.at[:, lanes], out_hbm.at[:, lanes], out_sems.at[step])
        copy.start()
        copies.append(copy)
    for copy in copies:
        copy.wait()
    send.wait()


VMEM = pl.BlockSpec(memory_space=pltpu.VMEM)


ANY = pl.BlockSpec(memory_space=pl.ANY)
MIB = 1024 * 1024


def shards(images, precision, rotation_offset, classes, prior_blocks):
    swap = [(0, 1), (1, 0)]
    other_images = lax.ppermute(images, "dom", swap)
    other_precision = lax.ppermute(precision, "dom", swap)
    other_offset = lax.ppermute(rotation_offset, "dom", swap)

    cost = pl.CostEstimate(flops=4 * 10**9, bytes_accessed=8 * MIB, transcendentals=36 * 104 * 128)
    cp, norm = pl.pallas_call(
        class_kernel,
        out_shape=(
            jax.ShapeDtypeStruct((RESIDUES, 2 * ROWS_16, COLS), jnp.bfloat16),
            jax.ShapeDtypeStruct((ROWS, LANES), jnp.float32),
        ),
        in_specs=[VMEM],
        out_specs=(VMEM,) * 2,
        compiler_params=pltpu.CompilerParams(vmem_limit_bytes=12 * MIB),
        cost_estimate=cost,
        name="classes",
    )(classes)

    e, by_residue, mine, tops = pl.pallas_call(
        score_kernel,
        out_shape=(
            jax.ShapeDtypeStruct((36, ROWS, COLS), jnp.float32),
            jax.ShapeDtypeStruct((COLS, RESIDUES * COLS), jnp.bfloat16),
            jax.ShapeDtypeStruct((16, COLS), jnp.float32),
            jax.ShapeDtypeStruct((ROWS, COLS), jnp.float32),
        ),
        in_specs=[VMEM] * 9,
        out_specs=(VMEM,) * 4,
        scratch_shapes=[
            pltpu.VMEM((36, ROWS, COLS), jnp.float32),
            pltpu.VMEM((ROWS, COLS), jnp.float32),
            pltpu.VMEM((40, COLS), jnp.float32),
        ],
        compiler_params=pltpu.CompilerParams(vmem_limit_bytes=20 * MIB),
        cost_estimate=cost,
        name="scores",
    )(
        prior_blocks,
        images,
        other_images,
        precision.reshape(1, OWN),
        other_precision.reshape(1, OWN),
        rotation_offset.reshape(1, OWN),
        other_offset.reshape(1, OWN),
        cp,
        norm,
    )
    theirs = lax.ppermute(mine, "dom", swap)

    weights = pl.pallas_call(
        spectrum_kernel,
        out_shape=jax.ShapeDtypeStruct((36, ROWS, COLS), jnp.float32),
        in_specs=[VMEM] * 3,
        out_specs=VMEM,
        compiler_params=pltpu.CompilerParams(vmem_limit_bytes=16 * MIB),
        cost_estimate=cost,
        name="spectra",
    )(e, tops, mine)

    parts = pl.pallas_call(
        sums_kernel,
        out_shape=jax.ShapeDtypeStruct((CHUNKS, QUADS, 4, LANES), jnp.float32),
        in_specs=[VMEM] * 4,
        out_specs=VMEM,
        scratch_shapes=[pltpu.VMEM((ROWS, RESIDUES * COLS), jnp.float32)],
        compiler_params=pltpu.CompilerParams(vmem_limit_bytes=20 * MIB),
        name="sums",
    )(weights, by_residue, mine, theirs)

    got = lax.all_to_all(parts.astype(jnp.float16), "cls", 0, 0, tiled=True)
    total = jnp.sum(got.astype(jnp.float32), axis=0).astype(jnp.float16)
    repeated = jnp.broadcast_to(total[None], (CHUNKS, QUADS, 4, LANES))
    whole = lax.all_to_all(repeated, "cls", 0, 0, tiled=True)
    new_classes, evidence = pl.pallas_call(
        finish_kernel,
        out_shape=(
            jax.ShapeDtypeStruct((CLASSES, BLOCKS * LANES), jnp.float32),
            jax.ShapeDtypeStruct((1, OWN), jnp.float32),
        ),
        in_specs=[VMEM] * 4,
        out_specs=(ANY, ANY),
        scratch_shapes=[
            pltpu.VMEM((CLASSES, BLOCKS * LANES), jnp.float32),
            pltpu.VMEM((1, OWN), jnp.float32),
            pltpu.SemaphoreType.DMA((FINISH_STEPS,)),
            pltpu.SemaphoreType.DMA,
        ],
        compiler_params=pltpu.CompilerParams(vmem_limit_bytes=12 * MIB),
        name="finish",
    )(whole.astype(jnp.float32).reshape(2, BLOCKS, QUADS, 4, LANES), classes, mine, theirs)
    return new_classes, evidence.reshape(OWN)


def solution(mesh):
    in_specs = (
        P(("cls", "dom"), None),
        P(("cls", "dom")),
        P(("cls", "dom")),
        P("dom", None),
        P("cls", "dom"),
    )
    out_specs = (P("dom", None), P(("cls", "dom")))
    return jax.shard_map(shards, mesh=mesh, in_specs=in_specs, out_specs=out_specs, check_vma=False)
```

```python
import math

import jax
import jax.numpy as jnp
import numpy as np
from jax import lax
from jax.experimental import pallas as pl
from jax.experimental.pallas import tpu as pltpu
from jax.sharding import PartitionSpec as P

FREQUENCIES = 64
CYCLES = 32
PART = FREQUENCIES * CYCLES
ROTATIONS = 36
CLASS_BLOCK = 5
EXCLUDED = -1e30
LOG2_E = math.log2(math.e)
PRIOR_WIDTH = 12.0
CLASS_PRIOR = 16.0

RESIDUES = 19
GROUP = 4
LANES = 128
OWN = 96
CLASSES = 100
ROWS = 104
ROWS_16 = 112
SPLIT = 48
HALF_ROWS = 52
QUADS = 13
COLS = 2 * LANES
CHUNKS = 64
BLOCKS = 32
SUM_SCALE = 0.25

SLOTS = [
    (0, 3), (1, 0, 3), (2, 1, 0), (3, 2, 1), (1, 3, 0), (1, 0, 3), (3, 1, 2), (0, 3, 1), (1, 3, 0), (2, 1, 0, 3),
    (3, 1, 0, 2), (0, 3, 2, 1), (3, 1, 2, 0), (0, 1, 2, 3), (1, 3, 2, 0), (2, 3, 0, 1), (1, 0, 3, 2), (2, 1, 0, 3), (3, 2),
]
PLACE = {}
for _j in range(RESIDUES):
    _same = [(m, 1) for m in range(FREQUENCIES) if m % ROTATIONS == _j]
    _back = [(m, -1) for m in range(FREQUENCIES) if m % ROTATIONS == (ROTATIONS - _j) % ROTATIONS and _j not in (0, 18)]
    for (_m, _sign), _slot in zip(_same + _back, SLOTS[_j], strict=True):
        PLACE[_m] = (_j, _slot, _sign)


def quarter_of(rows):
    return lax.broadcasted_iota(jnp.int32, (rows, LANES), 1) // CYCLES


class Rotated:
    def __init__(self, tile):
        self.tile, self.done = tile, {}

    def __call__(self, at, quarters):
        key = (at, quarters % GROUP)
        if key not in self.done:
            value = self(at, 0) if key[1] else self.tile(at)
            self.done[key] = pltpu.roll(value, key[1] * CYCLES, 1) if key[1] else value
        return self.done[key]


def by_quarter(pieces, quarter):
    whole = None
    for at, piece in pieces.items():
        if whole is None:
            whole = piece if len(pieces) == GROUP else jnp.where(quarter == at, piece, jnp.zeros_like(piece))
        else:
            whole = jnp.where(quarter == at, piece, whole)
    return whole


def to_residues(tile, rows):
    quarter = quarter_of(rows)
    rotated = Rotated(tile)
    for j in range(RESIDUES):
        pieces = {q: rotated(m // GROUP, q - m) for m, (i, q, _) in PLACE.items() if i == j}
        yield j, by_quarter(pieces, quarter)


def cosine(k):
    return float(np.cos(2.0 * np.pi * k / 9.0))


def sine(k):
    return float(np.sin(2.0 * np.pi * k / 9.0))


def nine_cos(x):
    c1, c2 = cosine(1), cosine(2)
    t, u = x[0] + x[3], (x[1] + x[2]) + x[4]
    base = x[0] - 0.5 * x[3]
    p, q = x[1] - x[4], x[2] - x[4]
    y1 = base + (p * c1 + q * c2)
    y2 = base + ((p - q) * c2 - q * c1)
    y4 = base - ((p - q) * c1 + p * c2)
    return [t + u, y1, y2, t - 0.5 * u, y4]


def nine_sin(x):
    s1, s3, s4 = sine(1), sine(3), sine(4)
    p, q = x[1] + x[2], x[2] + x[4]
    d = p - q
    t = x[3] * s3
    return [None, t + (p * s1 + q * s4), (d * s1 + p * s4) - t, ((x[1] - x[2]) + x[4]) * s3, t + (d * s4 - q * s1)]


def fold(j):
    j %= ROTATIONS
    return (j, 1) if j <= 18 else (ROTATIONS - j, -1)


def signed(values, j):
    at, sign = fold(j)
    return values[at] if sign > 0 else -values[at]


def rotation_of(r4, r9):
    return next(r for r in range(ROTATIONS) if r % 4 == r4 and r % 9 == r9)


def to_rotations(a, b):
    one = ([a[0]] + [a[fold(4 * k)[0]] for k in range(1, 5)], [None] + [signed(b, 4 * k) for k in range(1, 5)])
    alt = ([a[18]] + [a[fold(18 + 4 * k)[0]] for k in range(1, 5)], [None] + [signed(b, 18 + 4 * k) for k in range(1, 5)])
    cc, cs, sc, ss = [a[9]], [None], [b[9]], [None]
    for k in range(1, 5):
        a_p, b_p = a[fold(9 + 4 * k)[0]], b[fold(9 + 4 * k)[0]]
        a_m, b_m = a[fold(9 - 4 * k)[0]], b[fold(9 - 4 * k)[0]]
        assert fold(9 + 4 * k)[1] == fold(9 - 4 * k)[1]
        cc.append(a_p + a_m)
        ss.append(a_m - a_p)
        if fold(9 + 4 * k)[1] > 0:
            sc.append(b_p + b_m)
            cs.append(b_p - b_m)
        else:
            sc.append(-(b_p + b_m))
            cs.append(b_m - b_p)
    lines = []
    for even, odd in (one, alt, (cc, cs), (sc, ss)):
        e, o = nine_cos(even), nine_sin(odd)
        lines.append([e[0]] + [e[r] + o[r] for r in range(1, 5)] + [e[9 - r] - o[9 - r] for r in range(5, 9)])
    y = [None] * ROTATIONS
    for r9 in range(9):
        g1, gm, gc, gs = (line[r9] for line in lines)
        plus, minus = g1 + gm, g1 - gm
        y[rotation_of(0, r9)] = plus + gc
        y[rotation_of(2, r9)] = plus - gc
        y[rotation_of(1, r9)] = minus + gs
        y[rotation_of(3, r9)] = minus - gs
    return y


def from_rotations(e):
    lines = [[], [], [], []]
    for r9 in range(9):
        e0, e1, e2, e3 = (e[rotation_of(r4, r9)] for r4 in range(4))
        p, q = e0 + e2, e1 + e3
        for line, value in zip(lines, (p + q, p - q, e0 - e2, e1 - e3)):
            line.append(value)
    spectra = []
    for h in lines:
        even = [h[0]] + [h[k] + h[9 - k] for k in range(1, 5)]
        odd = [None] + [h[k] - h[9 - k] for k in range(1, 5)]
        spectra.append((nine_cos(even), nine_sin(odd)))
    (one_c, one_s), (alt_c, alt_s), (cc, cs), (sc, ss) = spectra
    c, s = [None] * RESIDUES, [None] * RESIDUES
    c[0], c[18], c[9], s[9] = one_c[0], alt_c[0], cc[0], sc[0]
    for k in range(1, 5):
        for first, cosines, sines in ((0, one_c, one_s), (18, alt_c, alt_s)):
            at, sign = fold(first + 4 * k)
            c[at], s[at] = cosines[k], sines[k] if sign > 0 else -sines[k]
        at_p, sign = fold(9 + 4 * k)
        at_m, _ = fold(9 - 4 * k)
        c[at_p], c[at_m] = cc[k] - ss[k], cc[k] + ss[k]
        if sign > 0:
            s[at_p], s[at_m] = sc[k] + cs[k], sc[k] - cs[k]
        else:
            s[at_p], s[at_m] = -(sc[k] + cs[k]), cs[k] - sc[k]
    return c, s


def sign_lanes(j, rows):
    quarter = quarter_of(rows)
    sign = jnp.ones((rows, LANES), jnp.float32)
    for i, q, direction in PLACE.values():
        if i == j and direction < 0:
            sign = jnp.where(quarter == q, -1.0, sign)
    return sign


def particle_row(values):
    return jnp.concatenate([values, jnp.zeros((1, LANES - OWN), values.dtype)], axis=1)


def score_kernel(blocks_ref, own_ref, other_ref, prec_a, prec_b, offset_a, offset_b, cp_ref, norm_ref, e_ref, xp_ref, stat_ref, top_ref, ab_ref, base_ref, prior_ref):
    blocks = CLASSES // CLASS_BLOCK
    first = lax.broadcasted_iota(jnp.int32, (ROWS, blocks), 1) * CLASS_BLOCK
    row = lax.broadcasted_iota(jnp.int32, (ROWS, blocks), 0)
    inside = (row >= first) & (row < first + CLASS_BLOCK)
    swapped = lax.axis_index("dom") == 1
    allowed = [blocks_ref[0:1], blocks_ref[1:2]]
    precisions = [particle_row(p[...].astype(jnp.float32) * LOG2_E) for p in (prec_a, prec_b)]
    for half in range(2):
        lanes = slice(half * LANES, (half + 1) * LANES)
        admit = jnp.where(swapped, allowed[1 - half], allowed[half]) == 1
        admit = jnp.sum(jnp.where(inside & admit, 1.0, 0.0), axis=1, keepdims=True)
        base_ref[:, lanes] = jnp.where(admit > 0.0, -0.5 * norm_ref[...] * precisions[half], EXCLUDED)
        offset = particle_row((offset_a, offset_b)[half][...])
        steps = lax.rem(lax.broadcasted_iota(jnp.int32, (40, LANES), 0) - offset + ROTATIONS, ROTATIONS)
        distance = jnp.minimum(steps, ROTATIONS - steps).astype(jnp.float32) * (1.0 / PRIOR_WIDTH)
        prior_ref[:, lanes] = (-0.5 * LOG2_E) * distance * distance
    zeros = jnp.zeros((LANES - OWN, RESIDUES * COLS), jnp.bfloat16)
    xp_ref[OWN:LANES] = zeros
    xp_ref[LANES + OWN :] = zeros
    for first_row, ref in ((0, own_ref), (LANES, other_ref)):
        for part in range(2):
            for i in range(0, OWN, 16):
                tiles = lambda t: ref[i : i + 16, part * PART + t * LANES : part * PART + (t + 1) * LANES]
                for j, value in to_residues(tiles, 16):
                    at = j * COLS + part * LANES
                    xp_ref[first_row + i : first_row + i + 16, at : at + LANES] = value
    for j in range(RESIDUES):
        pair = 0 < j < 18
        operand = cp_ref[j] if pair else cp_ref[j, :ROWS_16]
        got = lax.dot_general(
            operand, xp_ref[:, j * COLS : (j + 1) * COLS], (((1,), (1,)), ((), ())), preferred_element_type=jnp.float32
        )
        ab_ref[j] = got[:ROWS]
        if pair:
            ab_ref[18 + j] = got[ROWS_16 : ROWS_16 + ROWS]

    for half in range(2):
        lanes = slice(half * LANES, (half + 1) * LANES)
        prec = jnp.broadcast_to(precisions[half], (8, LANES))

        def scores(i, carry):
            peak, mass = carry
            rows = pl.ds(pl.multiple_of(i * 8, 8), 8)
            a = [ab_ref[j, rows, lanes] * prec for j in range(19)]
            b = [None] + [ab_ref[18 + j, rows, lanes] * prec for j in range(1, 18)]
            a[0] = a[0] + base_ref[rows, lanes]
            score = to_rotations(a, b)
            score = [score[r] + prior_ref[r : r + 1, lanes] for r in range(ROTATIONS)]
            top = score[0]
            for r in range(1, ROTATIONS):
                top = jnp.maximum(top, score[r])
            total = None
            for r in range(ROTATIONS):
                e = jnp.exp2(score[r] - top)
                e_ref[r, rows, lanes] = e
                total = e if total is None else total + e
            top_ref[rows, lanes] = top
            higher = jnp.maximum(peak, top)
            mass = mass * jnp.exp2(peak - higher) + total * jnp.exp2(top - higher)
            return higher, mass

        start = (jnp.full((8, LANES), EXCLUDED, jnp.float32), jnp.zeros((8, LANES), jnp.float32))
        tops, mass = lax.fori_loop(0, ROWS // 8, scores, start, unroll=True)
        peak = jnp.max(tops, axis=0, keepdims=True)
        mass = jnp.sum(mass * jnp.exp2(tops - peak), axis=0, keepdims=True)
        stat_ref[0:8, lanes] = jnp.broadcast_to(peak, (8, LANES))
        stat_ref[8:16, lanes] = jnp.broadcast_to(mass, (8, LANES))


def spectrum_kernel(e_ref, top_ref, stat_ref, w_ref):
    for half in range(2):
        lanes = slice(half * LANES, (half + 1) * LANES)

        peak = stat_ref[0:8, lanes]

        def spectra(i, carry):
            rows = pl.ds(pl.multiple_of(i * 8, 8), 8)
            lift = jnp.exp2(top_ref[rows, lanes] - peak)
            c, s = from_rotations([e_ref[r, rows, lanes] * lift for r in range(ROTATIONS)])
            for j in range(19):
                w_ref[j, rows, lanes] = c[j]
            for j in range(1, 18):
                w_ref[18 + j, rows, lanes] = s[j]
            return carry

        lax.fori_loop(0, ROWS // 8, spectra, 0, unroll=True)


def class_kernel(cls_ref, cp_ref, norm_ref):
    pad = jnp.zeros((ROWS_16 - CLASSES, LANES), jnp.bfloat16)
    for part in range(2):
        tiles = lambda t: cls_ref[:, part * PART + t * LANES : part * PART + (t + 1) * LANES]
        for j, value in to_residues(tiles, CLASSES):
            value = jnp.concatenate([value, pad], axis=0)
            cp_ref[j, :ROWS_16, part * LANES : (part + 1) * LANES] = value
            if 0 < j < 18:
                sign = sign_lanes(j, ROWS_16) * (1.0 if part else -1.0)
                cp_ref[j, ROWS_16:, (1 - part) * LANES : (2 - part) * LANES] = value * sign.astype(jnp.bfloat16)
    norm = jnp.zeros((CLASSES, LANES), jnp.float32)
    for block in range(BLOCKS):
        member = cls_ref[:, block * LANES : (block + 1) * LANES].astype(jnp.float32)
        norm = norm + member * member
    norm = jnp.broadcast_to(jnp.sum(norm, axis=1, keepdims=True), (CLASSES, LANES))
    norm_ref[...] = jnp.concatenate([norm, jnp.zeros((ROWS - CLASSES, LANES), jnp.float32)], axis=0)


def settle(mine, theirs, half):
    here = slice(half * LANES, (half + 1) * LANES)
    there = slice((1 - half) * LANES, (2 - half) * LANES)
    peak = jnp.maximum(mine[0:1, here], theirs[0:1, there])
    mass = mine[8:9, here] * jnp.exp2(mine[0:1, here] - peak)
    mass = mass + theirs[8:9, there] * jnp.exp2(theirs[0:1, there] - peak)
    held = lax.broadcasted_iota(jnp.int32, (1, LANES), 1) < OWN
    return held, peak, jnp.where(held, mass, 1.0)


def sums_kernel(w_ref, xp_ref, mine, theirs, out_ref, pc_ref):
    scale = []
    for half in range(2):
        held, peak, mass = settle(mine, theirs, half)
        lift = jnp.exp2(mine[0:1, half * LANES : (half + 1) * LANES] - peak)
        scale.append(jnp.where(held, lift * SUM_SCALE / mass, 0.0))
    scale = jnp.concatenate(scale, axis=1)

    def weights_of(i):
        return w_ref[i] * scale

    totals = weights_of(0)
    totals = jnp.concatenate([totals, jnp.zeros((LANES - ROWS, COLS), jnp.float32)], axis=0)
    high = totals.astype(jnp.bfloat16)
    low = (totals - high.astype(jnp.float32)).astype(jnp.bfloat16)
    ones = jnp.ones((16, COLS), jnp.bfloat16)
    dims = (((1,), (1,)), ((), ()))
    total = lax.dot_general(ones, high, dims, preferred_element_type=jnp.float32)
    total = total + lax.dot_general(ones, low, dims, preferred_element_type=jnp.float32)
    total = total[0:1]

    for j in range(RESIDUES):
        pair = 0 < j < 18
        weight = weights_of(j)
        if pair:
            weight = jnp.concatenate([weight, weights_of(18 + j)], axis=0)
        else:
            weight = jnp.concatenate([weight, jnp.zeros((8, COLS), jnp.float32)], axis=0)
        high = weight.astype(jnp.bfloat16)
        low = (weight - high.astype(jnp.float32)).astype(jnp.bfloat16)
        lanes = slice(j * COLS, (j + 1) * COLS)
        images = xp_ref[:, lanes]
        dims = (((1,), (0,)), ((), ()))
        got = lax.dot_general(high, images, dims, preferred_element_type=jnp.float32)
        got = got + lax.dot_general(low, images, dims, preferred_element_type=jnp.float32)
        re, im = got[:ROWS, :LANES], got[:ROWS, LANES:]
        if pair:
            sign = sign_lanes(j, ROWS)
            re, im = re - sign * got[ROWS:, LANES:], im + sign * got[ROWS:, :LANES]
        pc_ref[:, j * COLS : j * COLS + LANES] = re
        pc_ref[:, j * COLS + LANES : (j + 1) * COLS] = im

    quarter = quarter_of(8)
    last = jnp.broadcast_to(total, (4, LANES))
    for part in range(2):
        for i in range(ROWS // 8):
            rotated = Rotated(lambda j: pc_ref[i * 8 : (i + 1) * 8, j * COLS + part * LANES : j * COLS + (part + 1) * LANES])
            for t in range(BLOCKS // 2):
                pieces = {m % GROUP: rotated(PLACE[m][0], m - PLACE[m][1]) for m in range(t * GROUP, (t + 1) * GROUP)}
                value = by_quarter(pieces, quarter)
                half, at = divmod(i, SPLIT // 8) if i < ROWS // 8 - 1 else (1, i - SPLIT // 8)
                block = half * BLOCKS + part * (BLOCKS // 2) + t
                if i == ROWS // 8 - 1:
                    out_ref[block, QUADS - 1] = value[:4]
                else:
                    out_ref[block, 2 * at : 2 * at + 2] = value.reshape(2, 4, LANES)
                if half == 0 and at == 0:
                    out_ref[block, QUADS - 1] = last


FINISH_STEPS = 4
STEP_BLOCKS = BLOCKS // FINISH_STEPS


def finish_kernel(sum_ref, cls_ref, mine, theirs, out_hbm, evidence_hbm, out_ref, evidence_ref, out_sems, evidence_sem):
    _, peak, mass = settle(mine, theirs, 0)
    evidence_ref[...] = (peak * (1.0 / LOG2_E) + jnp.log(mass))[:, :OWN]
    send = pltpu.make_async_copy(evidence_ref, evidence_hbm, evidence_sem)
    send.start()
    row = lax.broadcasted_iota(jnp.int32, (HALF_ROWS, LANES), 0)
    lane = lax.broadcasted_iota(jnp.int32, (HALF_ROWS, LANES), 1)
    share = []
    total = sum_ref[0, 0, SPLIT // 4, 0:1, :]
    for half in range(2):
        weight = jnp.sum(jnp.where(lane == row + half * SPLIT, total, 0.0), axis=1, keepdims=True)
        share.append((1.0 / SUM_SCALE) / (weight * (1.0 / SUM_SCALE) + CLASS_PRIOR))
    copies = []
    for step in range(FINISH_STEPS):
        for block in range(step * STEP_BLOCKS, (step + 1) * STEP_BLOCKS):
            lanes = slice(block * LANES, (block + 1) * LANES)
            old = cls_ref[:, lanes].astype(jnp.float32)
            for half in range(2):
                count = SPLIT if half == 0 else CLASSES - SPLIT
                rows = slice(half * SPLIT, half * SPLIT + count)
                new = sum_ref[half, block].reshape(HALF_ROWS, LANES)[:count] + (CLASS_PRIOR * SUM_SCALE) * old[rows]
                out_ref[rows, lanes] = new * share[half][:count]
        lanes = slice(step * STEP_BLOCKS * LANES, (step + 1) * STEP_BLOCKS * LANES)
        copy = pltpu.make_async_copy(out_ref.at[:, lanes], out_hbm.at[:, lanes], out_sems.at[step])
        copy.start()
        copies.append(copy)
    for copy in copies:
        copy.wait()
    send.wait()


VMEM = pl.BlockSpec(memory_space=pltpu.VMEM)


ANY = pl.BlockSpec(memory_space=pl.ANY)
MIB = 1024 * 1024


def shards(images, precision, rotation_offset, classes, prior_blocks):
    swap = [(0, 1), (1, 0)]
    other_images = lax.ppermute(images, "dom", swap)
    other_precision = lax.ppermute(precision, "dom", swap)
    other_offset = lax.ppermute(rotation_offset, "dom", swap)

    cost = pl.CostEstimate(flops=4 * 10**9, bytes_accessed=8 * MIB, transcendentals=36 * 104 * 128)
    cp, norm = pl.pallas_call(
        class_kernel,
        out_shape=(
            jax.ShapeDtypeStruct((RESIDUES, 2 * ROWS_16, COLS), jnp.bfloat16),
            jax.ShapeDtypeStruct((ROWS, LANES), jnp.float32),
        ),
        in_specs=[VMEM],
        out_specs=(VMEM,) * 2,
        compiler_params=pltpu.CompilerParams(vmem_limit_bytes=12 * MIB),
        cost_estimate=cost,
        name="classes",
    )(classes)

    e, by_residue, mine, tops = pl.pallas_call(
        score_kernel,
        out_shape=(
            jax.ShapeDtypeStruct((36, ROWS, COLS), jnp.float32),
            jax.ShapeDtypeStruct((COLS, RESIDUES * COLS), jnp.bfloat16),
            jax.ShapeDtypeStruct((16, COLS), jnp.float32),
            jax.ShapeDtypeStruct((ROWS, COLS), jnp.float32),
        ),
        in_specs=[VMEM] * 9,
        out_specs=(VMEM,) * 4,
        scratch_shapes=[
            pltpu.VMEM((36, ROWS, COLS), jnp.float32),
            pltpu.VMEM((ROWS, COLS), jnp.float32),
            pltpu.VMEM((40, COLS), jnp.float32),
        ],
        compiler_params=pltpu.CompilerParams(vmem_limit_bytes=20 * MIB),
        cost_estimate=cost,
        name="scores",
    )(
        prior_blocks,
        images,
        other_images,
        precision.reshape(1, OWN),
        other_precision.reshape(1, OWN),
        rotation_offset.reshape(1, OWN),
        other_offset.reshape(1, OWN),
        cp,
        norm,
    )
    theirs = lax.ppermute(mine, "dom", swap)

    weights = pl.pallas_call(
        spectrum_kernel,
        out_shape=jax.ShapeDtypeStruct((36, ROWS, COLS), jnp.float32),
        in_specs=[VMEM] * 3,
        out_specs=VMEM,
        compiler_params=pltpu.CompilerParams(vmem_limit_bytes=16 * MIB),
        cost_estimate=cost,
        name="spectra",
    )(e, tops, mine)

    parts = pl.pallas_call(
        sums_kernel,
        out_shape=jax.ShapeDtypeStruct((CHUNKS, QUADS, 4, LANES), jnp.float32),
        in_specs=[VMEM] * 4,
        out_specs=VMEM,
        scratch_shapes=[pltpu.VMEM((ROWS, RESIDUES * COLS), jnp.float32)],
        compiler_params=pltpu.CompilerParams(vmem_limit_bytes=20 * MIB),
        name="sums",
    )(weights, by_residue, mine, theirs)

    got = lax.all_to_all(parts.reshape(CHUNKS * HALF_ROWS, LANES).astype(jnp.float16).reshape(parts.shape), "cls", 0, 0, tiled=True)
    total = jnp.sum(got.astype(jnp.float32), axis=0).astype(jnp.float16)
    repeated = jnp.broadcast_to(total[None], (CHUNKS, QUADS, 4, LANES))
    whole = lax.all_to_all(repeated, "cls", 0, 0, tiled=True)
    new_classes, evidence = pl.pallas_call(
        finish_kernel,
        out_shape=(
            jax.ShapeDtypeStruct((CLASSES, BLOCKS * LANES), jnp.float32),
            jax.ShapeDtypeStruct((1, OWN), jnp.float32),
        ),
        in_specs=[VMEM] * 4,
        out_specs=(ANY, ANY),
        scratch_shapes=[
            pltpu.VMEM((CLASSES, BLOCKS * LANES), jnp.float32),
            pltpu.VMEM((1, OWN), jnp.float32),
            pltpu.SemaphoreType.DMA((FINISH_STEPS,)),
            pltpu.SemaphoreType.DMA,
        ],
        compiler_params=pltpu.CompilerParams(vmem_limit_bytes=12 * MIB),
        name="finish",
    )(whole.reshape(CHUNKS * HALF_ROWS, LANES).astype(jnp.float32).reshape(2, BLOCKS, QUADS, 4, LANES), classes, mine, theirs)
    return new_classes, evidence.reshape(OWN)


def solution(mesh):
    in_specs = (
        P(("cls", "dom"), None),
        P(("cls", "dom")),
        P(("cls", "dom")),
        P("dom", None),
        P("cls", "dom"),
    )
    out_specs = (P("dom", None), P(("cls", "dom")))
    return jax.shard_map(shards, mesh=mesh, in_specs=in_specs, out_specs=out_specs, check_vma=False)
```

```python
import math

import jax
import jax.numpy as jnp
import numpy as np
from jax import lax
from jax.experimental import pallas as pl
from jax.experimental.pallas import tpu as pltpu
from jax.sharding import PartitionSpec as P

FREQUENCIES = 64
CYCLES = 32
PART = FREQUENCIES * CYCLES
ROTATIONS = 36
CLASS_BLOCK = 5
EXCLUDED = -1e30
LOG2_E = math.log2(math.e)
PRIOR_WIDTH = 12.0
CLASS_PRIOR = 16.0

RESIDUES = 19
GROUP = 4
LANES = 128
OWN = 96
CLASSES = 100
ROWS = 104
ROWS_16 = 112
SPLIT = 48
HALF_ROWS = 52
QUADS = 13
COLS = 2 * LANES
CHUNKS = 64
BLOCKS = 32
SUM_SCALE = 0.25

SLOTS = [
    (0, 3), (1, 0, 3), (2, 1, 0), (3, 2, 1), (1, 3, 0), (1, 0, 3), (3, 1, 2), (0, 3, 1), (1, 3, 0), (2, 1, 0, 3),
    (3, 1, 0, 2), (0, 3, 2, 1), (3, 1, 2, 0), (0, 1, 2, 3), (1, 3, 2, 0), (2, 3, 0, 1), (1, 0, 3, 2), (2, 1, 0, 3), (3, 2),
]
PLACE = {}
for _j in range(RESIDUES):
    _same = [(m, 1) for m in range(FREQUENCIES) if m % ROTATIONS == _j]
    _back = [(m, -1) for m in range(FREQUENCIES) if m % ROTATIONS == (ROTATIONS - _j) % ROTATIONS and _j not in (0, 18)]
    for (_m, _sign), _slot in zip(_same + _back, SLOTS[_j], strict=True):
        PLACE[_m] = (_j, _slot, _sign)


def quarter_of(rows):
    return lax.broadcasted_iota(jnp.int32, (rows, LANES), 1) // CYCLES


class Rotated:
    def __init__(self, tile):
        self.tile, self.done = tile, {}

    def __call__(self, at, quarters):
        key = (at, quarters % GROUP)
        if key not in self.done:
            value = self(at, 0) if key[1] else self.tile(at)
            self.done[key] = pltpu.roll(value, key[1] * CYCLES, 1) if key[1] else value
        return self.done[key]


def by_quarter(pieces, quarter):
    whole = None
    for at, piece in pieces.items():
        if whole is None:
            whole = piece if len(pieces) == GROUP else jnp.where(quarter == at, piece, jnp.zeros_like(piece))
        else:
            whole = jnp.where(quarter == at, piece, whole)
    return whole


def to_residues(tile, rows):
    quarter = quarter_of(rows)
    rotated = Rotated(tile)
    for j in range(RESIDUES):
        pieces = {q: rotated(m // GROUP, q - m) for m, (i, q, _) in PLACE.items() if i == j}
        yield j, by_quarter(pieces, quarter)


def cosine(k):
    return float(np.cos(2.0 * np.pi * k / 9.0))


def sine(k):
    return float(np.sin(2.0 * np.pi * k / 9.0))


def nine_cos(x):
    c1, c2 = cosine(1), cosine(2)
    t, u = x[0] + x[3], (x[1] + x[2]) + x[4]
    base = x[0] - 0.5 * x[3]
    p, q = x[1] - x[4], x[2] - x[4]
    y1 = base + (p * c1 + q * c2)
    y2 = base + ((p - q) * c2 - q * c1)
    y4 = base - ((p - q) * c1 + p * c2)
    return [t + u, y1, y2, t - 0.5 * u, y4]


def nine_sin(x):
    s1, s3, s4 = sine(1), sine(3), sine(4)
    p, q = x[1] + x[2], x[2] + x[4]
    d = p - q
    t = x[3] * s3
    return [None, t + (p * s1 + q * s4), (d * s1 + p * s4) - t, ((x[1] - x[2]) + x[4]) * s3, t + (d * s4 - q * s1)]


def fold(j):
    j %= ROTATIONS
    return (j, 1) if j <= 18 else (ROTATIONS - j, -1)


def signed(values, j):
    at, sign = fold(j)
    return values[at] if sign > 0 else -values[at]


def rotation_of(r4, r9):
    return next(r for r in range(ROTATIONS) if r % 4 == r4 and r % 9 == r9)


def to_rotations(a, b):
    one = ([a[0]] + [a[fold(4 * k)[0]] for k in range(1, 5)], [None] + [signed(b, 4 * k) for k in range(1, 5)])
    alt = ([a[18]] + [a[fold(18 + 4 * k)[0]] for k in range(1, 5)], [None] + [signed(b, 18 + 4 * k) for k in range(1, 5)])
    cc, cs, sc, ss = [a[9]], [None], [b[9]], [None]
    for k in range(1, 5):
        a_p, b_p = a[fold(9 + 4 * k)[0]], b[fold(9 + 4 * k)[0]]
        a_m, b_m = a[fold(9 - 4 * k)[0]], b[fold(9 - 4 * k)[0]]
        assert fold(9 + 4 * k)[1] == fold(9 - 4 * k)[1]
        cc.append(a_p + a_m)
        ss.append(a_m - a_p)
        if fold(9 + 4 * k)[1] > 0:
            sc.append(b_p + b_m)
            cs.append(b_p - b_m)
        else:
            sc.append(-(b_p + b_m))
            cs.append(b_m - b_p)
    lines = []
    for even, odd in (one, alt, (cc, cs), (sc, ss)):
        e, o = nine_cos(even), nine_sin(odd)
        lines.append([e[0]] + [e[r] + o[r] for r in range(1, 5)] + [e[9 - r] - o[9 - r] for r in range(5, 9)])
    y = [None] * ROTATIONS
    for r9 in range(9):
        g1, gm, gc, gs = (line[r9] for line in lines)
        plus, minus = g1 + gm, g1 - gm
        y[rotation_of(0, r9)] = plus + gc
        y[rotation_of(2, r9)] = plus - gc
        y[rotation_of(1, r9)] = minus + gs
        y[rotation_of(3, r9)] = minus - gs
    return y


def from_rotations(e):
    lines = [[], [], [], []]
    for r9 in range(9):
        e0, e1, e2, e3 = (e[rotation_of(r4, r9)] for r4 in range(4))
        p, q = e0 + e2, e1 + e3
        for line, value in zip(lines, (p + q, p - q, e0 - e2, e1 - e3)):
            line.append(value)
    spectra = []
    for h in lines:
        even = [h[0]] + [h[k] + h[9 - k] for k in range(1, 5)]
        odd = [None] + [h[k] - h[9 - k] for k in range(1, 5)]
        spectra.append((nine_cos(even), nine_sin(odd)))
    (one_c, one_s), (alt_c, alt_s), (cc, cs), (sc, ss) = spectra
    c, s = [None] * RESIDUES, [None] * RESIDUES
    c[0], c[18], c[9], s[9] = one_c[0], alt_c[0], cc[0], sc[0]
    for k in range(1, 5):
        for first, cosines, sines in ((0, one_c, one_s), (18, alt_c, alt_s)):
            at, sign = fold(first + 4 * k)
            c[at], s[at] = cosines[k], sines[k] if sign > 0 else -sines[k]
        at_p, sign = fold(9 + 4 * k)
        at_m, _ = fold(9 - 4 * k)
        c[at_p], c[at_m] = cc[k] - ss[k], cc[k] + ss[k]
        if sign > 0:
            s[at_p], s[at_m] = sc[k] + cs[k], sc[k] - cs[k]
        else:
            s[at_p], s[at_m] = -(sc[k] + cs[k]), cs[k] - sc[k]
    return c, s


def sign_lanes(j, rows):
    quarter = quarter_of(rows)
    sign = jnp.ones((rows, LANES), jnp.float32)
    for i, q, direction in PLACE.values():
        if i == j and direction < 0:
            sign = jnp.where(quarter == q, -1.0, sign)
    return sign


def particle_row(values):
    return jnp.concatenate([values, jnp.zeros((1, LANES - OWN), values.dtype)], axis=1)


def correlate(image_ref, cp_ref, xp_ref, ab_ref):
    xp_ref[OWN:] = jnp.zeros((LANES - OWN, RESIDUES * COLS), jnp.bfloat16)
    for part in range(2):
        for i in range(0, OWN, 16):
            tiles = lambda t: image_ref[i : i + 16, part * PART + t * LANES : part * PART + (t + 1) * LANES]
            for j, value in to_residues(tiles, 16):
                at = j * COLS + part * LANES
                xp_ref[i : i + 16, at : at + LANES] = value
    for j in range(RESIDUES):
        pair = 0 < j < 18
        operand = cp_ref[j] if pair else cp_ref[j, :ROWS_16]
        got = lax.dot_general(
            operand, xp_ref[:, j * COLS : (j + 1) * COLS], (((1,), (1,)), ((), ())), preferred_element_type=jnp.float32
        )
        ab_ref[j] = got[:ROWS]
        if pair:
            ab_ref[18 + j] = got[ROWS_16 : ROWS_16 + ROWS]


def score_kernel(blocks_ref, other_ref, prec_a, prec_b, offset_a, offset_b, cp_ref, norm_ref, ab_own, e_ref, xp_ref, stat_ref, top_ref, ab_other, base_ref, prior_ref):
    blocks = CLASSES // CLASS_BLOCK
    first = lax.broadcasted_iota(jnp.int32, (ROWS, blocks), 1) * CLASS_BLOCK
    row = lax.broadcasted_iota(jnp.int32, (ROWS, blocks), 0)
    inside = (row >= first) & (row < first + CLASS_BLOCK)
    swapped = lax.axis_index("dom") == 1
    allowed = [blocks_ref[0:1], blocks_ref[1:2]]
    precisions = [particle_row(p[...].astype(jnp.float32) * LOG2_E) for p in (prec_a, prec_b)]
    for half in range(2):
        lanes = slice(half * LANES, (half + 1) * LANES)
        admit = jnp.where(swapped, allowed[1 - half], allowed[half]) == 1
        admit = jnp.sum(jnp.where(inside & admit, 1.0, 0.0), axis=1, keepdims=True)
        base_ref[:, lanes] = jnp.where(admit > 0.0, -0.5 * norm_ref[...] * precisions[half], EXCLUDED)
        offset = particle_row((offset_a, offset_b)[half][...])
        steps = lax.rem(lax.broadcasted_iota(jnp.int32, (40, LANES), 0) - offset + ROTATIONS, ROTATIONS)
        distance = jnp.minimum(steps, ROTATIONS - steps).astype(jnp.float32) * (1.0 / PRIOR_WIDTH)
        prior_ref[:, lanes] = (-0.5 * LOG2_E) * distance * distance
    correlate(other_ref, cp_ref, xp_ref, ab_other)

    for half in range(2):
        lanes = slice(half * LANES, (half + 1) * LANES)
        prec = jnp.broadcast_to(precisions[half], (8, LANES))
        ab_ref = (ab_own, ab_other)[half]

        def scores(i, carry):
            peak, mass = carry
            rows = pl.ds(pl.multiple_of(i * 8, 8), 8)
            a = [ab_ref[j, rows] * prec for j in range(19)]
            b = [None] + [ab_ref[18 + j, rows] * prec for j in range(1, 18)]
            a[0] = a[0] + base_ref[rows, lanes]
            score = to_rotations(a, b)
            score = [score[r] + prior_ref[r : r + 1, lanes] for r in range(ROTATIONS)]
            top = score[0]
            for r in range(1, ROTATIONS):
                top = jnp.maximum(top, score[r])
            total = None
            for r in range(ROTATIONS):
                e = jnp.exp2(score[r] - top)
                e_ref[r, rows, lanes] = e
                total = e if total is None else total + e
            top_ref[rows, lanes] = top
            higher = jnp.maximum(peak, top)
            mass = mass * jnp.exp2(peak - higher) + total * jnp.exp2(top - higher)
            return higher, mass

        start = (jnp.full((8, LANES), EXCLUDED, jnp.float32), jnp.zeros((8, LANES), jnp.float32))
        tops, mass = lax.fori_loop(0, ROWS // 8, scores, start, unroll=True)
        peak = jnp.max(tops, axis=0, keepdims=True)
        mass = jnp.sum(mass * jnp.exp2(tops - peak), axis=0, keepdims=True)
        stat_ref[0:8, lanes] = jnp.broadcast_to(peak, (8, LANES))
        stat_ref[8:16, lanes] = jnp.broadcast_to(mass, (8, LANES))


def spectrum_kernel(e_ref, top_ref, stat_ref, w_ref):
    for half in range(2):
        lanes = slice(half * LANES, (half + 1) * LANES)

        peak = stat_ref[0:8, lanes]

        def spectra(i, carry):
            rows = pl.ds(pl.multiple_of(i * 8, 8), 8)
            lift = jnp.exp2(top_ref[rows, lanes] - peak)
            c, s = from_rotations([e_ref[r, rows, lanes] * lift for r in range(ROTATIONS)])
            for j in range(19):
                w_ref[j, rows, lanes] = c[j]
            for j in range(1, 18):
                w_ref[18 + j, rows, lanes] = s[j]
            return carry

        lax.fori_loop(0, ROWS // 8, spectra, 0, unroll=True)


def sign_kernel(sign_ref):
    for j in range(RESIDUES):
        sign_ref[j : j + 1] = sign_lanes(j, 1)


def own_kernel(cls_ref, sign_ref, own_ref, cp_ref, norm_ref, xp_ref, ab_ref):
    pad = jnp.zeros((ROWS_16 - CLASSES, LANES), jnp.bfloat16)
    for part in range(2):
        tiles = lambda t: cls_ref[:, part * PART + t * LANES : part * PART + (t + 1) * LANES]
        for j, value in to_residues(tiles, CLASSES):
            value = jnp.concatenate([value, pad], axis=0)
            cp_ref[j, :ROWS_16, part * LANES : (part + 1) * LANES] = value
            if 0 < j < 18:
                sign = jnp.broadcast_to(sign_ref[j : j + 1], (ROWS_16, LANES)) * (1.0 if part else -1.0)
                cp_ref[j, ROWS_16:, (1 - part) * LANES : (2 - part) * LANES] = value * sign.astype(jnp.bfloat16)
    norm = jnp.zeros((CLASSES, LANES), jnp.float32)
    for block in range(BLOCKS):
        member = cls_ref[:, block * LANES : (block + 1) * LANES].astype(jnp.float32)
        norm = norm + member * member
    norm = jnp.broadcast_to(jnp.sum(norm, axis=1, keepdims=True), (CLASSES, LANES))
    norm_ref[...] = jnp.concatenate([norm, jnp.zeros((ROWS - CLASSES, LANES), jnp.float32)], axis=0)
    correlate(own_ref, cp_ref, xp_ref, ab_ref)


def settle(mine, theirs, half):
    here = slice(half * LANES, (half + 1) * LANES)
    there = slice((1 - half) * LANES, (2 - half) * LANES)
    peak = jnp.maximum(mine[0:1, here], theirs[0:1, there])
    mass = mine[8:9, here] * jnp.exp2(mine[0:1, here] - peak)
    mass = mass + theirs[8:9, there] * jnp.exp2(theirs[0:1, there] - peak)
    held = lax.broadcasted_iota(jnp.int32, (1, LANES), 1) < OWN
    return held, peak, jnp.where(held, mass, 1.0)


def sums_kernel(w_ref, xp_own, xp_other, mine, theirs, out_ref, pc_ref):
    scale = []
    for half in range(2):
        held, peak, mass = settle(mine, theirs, half)
        lift = jnp.exp2(mine[0:1, half * LANES : (half + 1) * LANES] - peak)
        scale.append(jnp.where(held, lift * SUM_SCALE / mass, 0.0))
    scale = jnp.concatenate(scale, axis=1)

    def weights_of(i):
        return w_ref[i] * scale

    totals = weights_of(0)
    totals = jnp.concatenate([totals, jnp.zeros((LANES - ROWS, COLS), jnp.float32)], axis=0)
    high = totals.astype(jnp.bfloat16)
    low = (totals - high.astype(jnp.float32)).astype(jnp.bfloat16)
    ones = jnp.ones((16, COLS), jnp.bfloat16)
    dims = (((1,), (1,)), ((), ()))
    total = lax.dot_general(ones, high, dims, preferred_element_type=jnp.float32)
    total = total + lax.dot_general(ones, low, dims, preferred_element_type=jnp.float32)
    total = total[0:1]

    for j in range(RESIDUES):
        pair = 0 < j < 18
        weight = weights_of(j)
        if pair:
            weight = jnp.concatenate([weight, weights_of(18 + j)], axis=0)
        else:
            weight = jnp.concatenate([weight, jnp.zeros((8, COLS), jnp.float32)], axis=0)
        high = weight.astype(jnp.bfloat16)
        low = (weight - high.astype(jnp.float32)).astype(jnp.bfloat16)
        lanes = slice(j * COLS, (j + 1) * COLS)
        images = jnp.concatenate([xp_own[:, lanes], xp_other[:, lanes]], axis=0)
        dims = (((1,), (0,)), ((), ()))
        got = lax.dot_general(high, images, dims, preferred_element_type=jnp.float32)
        got = got + lax.dot_general(low, images, dims, preferred_element_type=jnp.float32)
        re, im = got[:ROWS, :LANES], got[:ROWS, LANES:]
        if pair:
            sign = sign_lanes(j, ROWS)
            re, im = re - sign * got[ROWS:, LANES:], im + sign * got[ROWS:, :LANES]
        pc_ref[:, j * COLS : j * COLS + LANES] = re
        pc_ref[:, j * COLS + LANES : (j + 1) * COLS] = im

    quarter = quarter_of(8)
    last = jnp.broadcast_to(total, (4, LANES))
    for part in range(2):
        for i in range(ROWS // 8):
            rotated = Rotated(lambda j: pc_ref[i * 8 : (i + 1) * 8, j * COLS + part * LANES : j * COLS + (part + 1) * LANES])
            for t in range(BLOCKS // 2):
                pieces = {m % GROUP: rotated(PLACE[m][0], m - PLACE[m][1]) for m in range(t * GROUP, (t + 1) * GROUP)}
                value = by_quarter(pieces, quarter)
                half, at = divmod(i, SPLIT // 8) if i < ROWS // 8 - 1 else (1, i - SPLIT // 8)
                block = half * BLOCKS + part * (BLOCKS // 2) + t
                if i == ROWS // 8 - 1:
                    out_ref[block, QUADS - 1] = value[:4]
                else:
                    out_ref[block, 2 * at : 2 * at + 2] = value.reshape(2, 4, LANES)
                if half == 0 and at == 0:
                    out_ref[block, QUADS - 1] = last


FINISH_STEPS = 4
STEP_BLOCKS = BLOCKS // FINISH_STEPS


def finish_kernel(sum_ref, cls_ref, mine, theirs, out_hbm, evidence_hbm, out_ref, evidence_ref, out_sems, evidence_sem):
    _, peak, mass = settle(mine, theirs, 0)
    evidence_ref[...] = (peak * (1.0 / LOG2_E) + jnp.log(mass))[:, :OWN]
    send = pltpu.make_async_copy(evidence_ref, evidence_hbm, evidence_sem)
    send.start()
    row = lax.broadcasted_iota(jnp.int32, (HALF_ROWS, LANES), 0)
    lane = lax.broadcasted_iota(jnp.int32, (HALF_ROWS, LANES), 1)
    share = []
    total = sum_ref[0, 0, SPLIT // 4, 0:1, :]
    for half in range(2):
        weight = jnp.sum(jnp.where(lane == row + half * SPLIT, total, 0.0), axis=1, keepdims=True)
        share.append((1.0 / SUM_SCALE) / (weight * (1.0 / SUM_SCALE) + CLASS_PRIOR))
    copies = []
    for step in range(FINISH_STEPS):
        for block in range(step * STEP_BLOCKS, (step + 1) * STEP_BLOCKS):
            lanes = slice(block * LANES, (block + 1) * LANES)
            old = cls_ref[:, lanes].astype(jnp.float32)
            for half in range(2):
                count = SPLIT if half == 0 else CLASSES - SPLIT
                rows = slice(half * SPLIT, half * SPLIT + count)
                new = sum_ref[half, block].reshape(HALF_ROWS, LANES)[:count] + (CLASS_PRIOR * SUM_SCALE) * old[rows]
                out_ref[rows, lanes] = new * share[half][:count]
        lanes = slice(step * STEP_BLOCKS * LANES, (step + 1) * STEP_BLOCKS * LANES)
        copy = pltpu.make_async_copy(out_ref.at[:, lanes], out_hbm.at[:, lanes], out_sems.at[step])
        copy.start()
        copies.append(copy)
    for copy in copies:
        copy.wait()
    send.wait()


VMEM = pl.BlockSpec(memory_space=pltpu.VMEM)


ANY = pl.BlockSpec(memory_space=pl.ANY)
MIB = 1024 * 1024


def shards(images, precision, rotation_offset, classes, prior_blocks):
    swap = [(0, 1), (1, 0)]
    other_images = lax.ppermute(images, "dom", swap)
    other_precision = lax.ppermute(precision, "dom", swap)
    other_offset = lax.ppermute(rotation_offset, "dom", swap)

    cost = pl.CostEstimate(flops=4 * 10**9, bytes_accessed=8 * MIB, transcendentals=36 * 104 * 128)
    signs = pl.pallas_call(
        sign_kernel,
        out_shape=jax.ShapeDtypeStruct((RESIDUES, LANES), jnp.float32),
        out_specs=VMEM,
        compiler_params=pltpu.CompilerParams(vmem_limit_bytes=4 * MIB),
        cost_estimate=cost,
        name="signs",
    )()
    cp, norm, xp_own, ab_own = pl.pallas_call(
        own_kernel,
        out_shape=(
            jax.ShapeDtypeStruct((RESIDUES, 2 * ROWS_16, COLS), jnp.bfloat16),
            jax.ShapeDtypeStruct((ROWS, LANES), jnp.float32),
            jax.ShapeDtypeStruct((LANES, RESIDUES * COLS), jnp.bfloat16),
            jax.ShapeDtypeStruct((36, ROWS, LANES), jnp.float32),
        ),
        in_specs=[VMEM] * 3,
        out_specs=(VMEM,) * 4,
        compiler_params=pltpu.CompilerParams(vmem_limit_bytes=16 * MIB),
        cost_estimate=cost,
        name="own",
    )(classes, signs, images)

    e, xp_other, mine, tops = pl.pallas_call(
        score_kernel,
        out_shape=(
            jax.ShapeDtypeStruct((36, ROWS, COLS), jnp.float32),
            jax.ShapeDtypeStruct((LANES, RESIDUES * COLS), jnp.bfloat16),
            jax.ShapeDtypeStruct((16, COLS), jnp.float32),
            jax.ShapeDtypeStruct((ROWS, COLS), jnp.float32),
        ),
        in_specs=[VMEM] * 9,
        out_specs=(VMEM,) * 4,
        scratch_shapes=[
            pltpu.VMEM((36, ROWS, LANES), jnp.float32),
            pltpu.VMEM((ROWS, COLS), jnp.float32),
            pltpu.VMEM((40, COLS), jnp.float32),
        ],
        compiler_params=pltpu.CompilerParams(vmem_limit_bytes=20 * MIB),
        cost_estimate=cost,
        name="scores",
    )(
        prior_blocks,
        other_images,
        precision.reshape(1, OWN),
        other_precision.reshape(1, OWN),
        rotation_offset.reshape(1, OWN),
        other_offset.reshape(1, OWN),
        cp,
        norm,
        ab_own,
    )
    theirs = lax.ppermute(mine, "dom", swap)

    weights = pl.pallas_call(
        spectrum_kernel,
        out_shape=jax.ShapeDtypeStruct((36, ROWS, COLS), jnp.float32),
        in_specs=[VMEM] * 3,
        out_specs=VMEM,
        compiler_params=pltpu.CompilerParams(vmem_limit_bytes=16 * MIB),
        cost_estimate=cost,
        name="spectra",
    )(e, tops, mine)

    parts = pl.pallas_call(
        sums_kernel,
        out_shape=jax.ShapeDtypeStruct((CHUNKS, QUADS, 4, LANES), jnp.float32),
        in_specs=[VMEM] * 5,
        out_specs=VMEM,
        scratch_shapes=[pltpu.VMEM((ROWS, RESIDUES * COLS), jnp.float32)],
        compiler_params=pltpu.CompilerParams(vmem_limit_bytes=20 * MIB),
        name="sums",
    )(weights, xp_own, xp_other, mine, theirs)

    flat = lax.optimization_barrier(parts.reshape(CHUNKS * HALF_ROWS, LANES))
    flat = lax.optimization_barrier(flat.astype(jnp.float16))
    got = lax.all_to_all(flat.reshape(parts.shape), "cls", 0, 0, tiled=True)
    total = jnp.sum(got.astype(jnp.float32), axis=0).astype(jnp.float16)
    repeated = jnp.broadcast_to(total[None], (CHUNKS, QUADS, 4, LANES))
    whole = lax.all_to_all(repeated, "cls", 0, 0, tiled=True)
    new_classes, evidence = pl.pallas_call(
        finish_kernel,
        out_shape=(
            jax.ShapeDtypeStruct((CLASSES, BLOCKS * LANES), jnp.float32),
            jax.ShapeDtypeStruct((1, OWN), jnp.float32),
        ),
        in_specs=[VMEM] * 4,
        out_specs=(ANY, ANY),
        scratch_shapes=[
            pltpu.VMEM((CLASSES, BLOCKS * LANES), jnp.float32),
            pltpu.VMEM((1, OWN), jnp.float32),
            pltpu.SemaphoreType.DMA((FINISH_STEPS,)),
            pltpu.SemaphoreType.DMA,
        ],
        compiler_params=pltpu.CompilerParams(vmem_limit_bytes=12 * MIB),
        name="finish",
    )(lax.optimization_barrier(lax.optimization_barrier(whole.reshape(CHUNKS * HALF_ROWS, LANES)).astype(jnp.float32)).reshape(2, BLOCKS, QUADS, 4, LANES), classes, mine, theirs)
    return new_classes, evidence.reshape(OWN)


def solution(mesh):
    in_specs = (
        P(("cls", "dom"), None),
        P(("cls", "dom")),
        P(("cls", "dom")),
        P("dom", None),
        P("cls", "dom"),
    )
    out_specs = (P("dom", None), P(("cls", "dom")))
    return jax.shard_map(shards, mesh=mesh, in_specs=in_specs, out_specs=out_specs, check_vma=False)
```

```python
import math

import jax
import jax.numpy as jnp
import numpy as np
from jax import lax
from jax.experimental import pallas as pl
from jax.experimental.pallas import tpu as pltpu
from jax.sharding import PartitionSpec as P

FREQUENCIES = 64
CYCLES = 32
PART = FREQUENCIES * CYCLES
ROTATIONS = 36
CLASS_BLOCK = 5
EXCLUDED = -1e30
LOG2_E = math.log2(math.e)
PRIOR_WIDTH = 12.0
CLASS_PRIOR = 16.0

RESIDUES = 19
GROUP = 4
LANES = 128
OWN = 96
CLASSES = 100
ROWS = 104
ROWS_16 = 112
SPLIT = 48
HALF_ROWS = 52
QUADS = 13
COLS = 2 * LANES
CHUNKS = 64
BLOCKS = 32
SUM_SCALE = 0.25

SLOTS = [
    (0, 3), (1, 0, 3), (2, 1, 0), (3, 2, 1), (1, 3, 0), (1, 0, 3), (3, 1, 2), (0, 3, 1), (1, 3, 0), (2, 1, 0, 3),
    (3, 1, 0, 2), (0, 3, 2, 1), (3, 1, 2, 0), (0, 1, 2, 3), (1, 3, 2, 0), (2, 3, 0, 1), (1, 0, 3, 2), (2, 1, 0, 3), (3, 2),
]
PLACE = {}
for _j in range(RESIDUES):
    _same = [(m, 1) for m in range(FREQUENCIES) if m % ROTATIONS == _j]
    _back = [(m, -1) for m in range(FREQUENCIES) if m % ROTATIONS == (ROTATIONS - _j) % ROTATIONS and _j not in (0, 18)]
    for (_m, _sign), _slot in zip(_same + _back, SLOTS[_j], strict=True):
        PLACE[_m] = (_j, _slot, _sign)


def quarter_of(rows):
    return lax.broadcasted_iota(jnp.int32, (rows, LANES), 1) // CYCLES


class Rotated:
    def __init__(self, tile):
        self.tile, self.done = tile, {}

    def __call__(self, at, quarters):
        key = (at, quarters % GROUP)
        if key not in self.done:
            value = self(at, 0) if key[1] else self.tile(at)
            self.done[key] = pltpu.roll(value, key[1] * CYCLES, 1) if key[1] else value
        return self.done[key]


def by_quarter(pieces, quarter):
    whole = None
    for at, piece in pieces.items():
        if whole is None:
            whole = piece if len(pieces) == GROUP else jnp.where(quarter == at, piece, jnp.zeros_like(piece))
        else:
            whole = jnp.where(quarter == at, piece, whole)
    return whole


def to_residues(tile, rows):
    quarter = quarter_of(rows)
    rotated = Rotated(tile)
    for j in range(RESIDUES):
        pieces = {q: rotated(m // GROUP, q - m) for m, (i, q, _) in PLACE.items() if i == j}
        yield j, by_quarter(pieces, quarter)


def cosine(k):
    return float(np.cos(2.0 * np.pi * k / 9.0))


def sine(k):
    return float(np.sin(2.0 * np.pi * k / 9.0))


def nine_cos(x):
    c1, c2 = cosine(1), cosine(2)
    t, u = x[0] + x[3], (x[1] + x[2]) + x[4]
    base = x[0] - 0.5 * x[3]
    p, q = x[1] - x[4], x[2] - x[4]
    y1 = base + (p * c1 + q * c2)
    y2 = base + ((p - q) * c2 - q * c1)
    y4 = base - ((p - q) * c1 + p * c2)
    return [t + u, y1, y2, t - 0.5 * u, y4]


def nine_sin(x):
    s1, s3, s4 = sine(1), sine(3), sine(4)
    p, q = x[1] + x[2], x[2] + x[4]
    d = p - q
    t = x[3] * s3
    return [None, t + (p * s1 + q * s4), (d * s1 + p * s4) - t, ((x[1] - x[2]) + x[4]) * s3, t + (d * s4 - q * s1)]


def fold(j):
    j %= ROTATIONS
    return (j, 1) if j <= 18 else (ROTATIONS - j, -1)


def signed(values, j):
    at, sign = fold(j)
    return values[at] if sign > 0 else -values[at]


def rotation_of(r4, r9):
    return next(r for r in range(ROTATIONS) if r % 4 == r4 and r % 9 == r9)


def to_rotations(a, b):
    one = ([a[0]] + [a[fold(4 * k)[0]] for k in range(1, 5)], [None] + [signed(b, 4 * k) for k in range(1, 5)])
    alt = ([a[18]] + [a[fold(18 + 4 * k)[0]] for k in range(1, 5)], [None] + [signed(b, 18 + 4 * k) for k in range(1, 5)])
    cc, cs, sc, ss = [a[9]], [None], [b[9]], [None]
    for k in range(1, 5):
        a_p, b_p = a[fold(9 + 4 * k)[0]], b[fold(9 + 4 * k)[0]]
        a_m, b_m = a[fold(9 - 4 * k)[0]], b[fold(9 - 4 * k)[0]]
        assert fold(9 + 4 * k)[1] == fold(9 - 4 * k)[1]
        cc.append(a_p + a_m)
        ss.append(a_m - a_p)
        if fold(9 + 4 * k)[1] > 0:
            sc.append(b_p + b_m)
            cs.append(b_p - b_m)
        else:
            sc.append(-(b_p + b_m))
            cs.append(b_m - b_p)
    lines = []
    for even, odd in (one, alt, (cc, cs), (sc, ss)):
        e, o = nine_cos(even), nine_sin(odd)
        lines.append([e[0]] + [e[r] + o[r] for r in range(1, 5)] + [e[9 - r] - o[9 - r] for r in range(5, 9)])
    y = [None] * ROTATIONS
    for r9 in range(9):
        g1, gm, gc, gs = (line[r9] for line in lines)
        plus, minus = g1 + gm, g1 - gm
        y[rotation_of(0, r9)] = plus + gc
        y[rotation_of(2, r9)] = plus - gc
        y[rotation_of(1, r9)] = minus + gs
        y[rotation_of(3, r9)] = minus - gs
    return y


def from_rotations(e):
    lines = [[], [], [], []]
    for r9 in range(9):
        e0, e1, e2, e3 = (e[rotation_of(r4, r9)] for r4 in range(4))
        p, q = e0 + e2, e1 + e3
        for line, value in zip(lines, (p + q, p - q, e0 - e2, e1 - e3)):
            line.append(value)
    spectra = []
    for h in lines:
        even = [h[0]] + [h[k] + h[9 - k] for k in range(1, 5)]
        odd = [None] + [h[k] - h[9 - k] for k in range(1, 5)]
        spectra.append((nine_cos(even), nine_sin(odd)))
    (one_c, one_s), (alt_c, alt_s), (cc, cs), (sc, ss) = spectra
    c, s = [None] * RESIDUES, [None] * RESIDUES
    c[0], c[18], c[9], s[9] = one_c[0], alt_c[0], cc[0], sc[0]
    for k in range(1, 5):
        for first, cosines, sines in ((0, one_c, one_s), (18, alt_c, alt_s)):
            at, sign = fold(first + 4 * k)
            c[at], s[at] = cosines[k], sines[k] if sign > 0 else -sines[k]
        at_p, sign = fold(9 + 4 * k)
        at_m, _ = fold(9 - 4 * k)
        c[at_p], c[at_m] = cc[k] - ss[k], cc[k] + ss[k]
        if sign > 0:
            s[at_p], s[at_m] = sc[k] + cs[k], sc[k] - cs[k]
        else:
            s[at_p], s[at_m] = -(sc[k] + cs[k]), cs[k] - sc[k]
    return c, s


def sign_lanes(j, rows):
    quarter = quarter_of(rows)
    sign = jnp.ones((rows, LANES), jnp.float32)
    for i, q, direction in PLACE.values():
        if i == j and direction < 0:
            sign = jnp.where(quarter == q, -1.0, sign)
    return sign


def particle_row(values):
    return jnp.concatenate([values, jnp.zeros((1, LANES - OWN), values.dtype)], axis=1)


def correlate(image_ref, cp_ref, xp_ref, ab_ref):
    xp_ref[OWN:] = jnp.zeros((LANES - OWN, RESIDUES * COLS), jnp.bfloat16)
    for part in range(2):
        for i in range(0, OWN, 16):
            tiles = lambda t: image_ref[i : i + 16, part * PART + t * LANES : part * PART + (t + 1) * LANES]
            for j, value in to_residues(tiles, 16):
                at = j * COLS + part * LANES
                xp_ref[i : i + 16, at : at + LANES] = value
    for j in range(RESIDUES):
        pair = 0 < j < 18
        operand = cp_ref[j] if pair else cp_ref[j, :ROWS_16]
        got = lax.dot_general(
            operand, xp_ref[:, j * COLS : (j + 1) * COLS], (((1,), (1,)), ((), ())), preferred_element_type=jnp.float32
        )
        ab_ref[j] = got[:ROWS]
        if pair:
            ab_ref[18 + j] = got[ROWS_16 : ROWS_16 + ROWS]


def score_kernel(blocks_ref, other_ref, prec_a, prec_b, offset_a, offset_b, cp_ref, norm_ref, ab_own, e_ref, xp_ref, stat_ref, top_ref, ab_other, base_ref, prior_ref):
    blocks = CLASSES // CLASS_BLOCK
    first = lax.broadcasted_iota(jnp.int32, (ROWS, blocks), 1) * CLASS_BLOCK
    row = lax.broadcasted_iota(jnp.int32, (ROWS, blocks), 0)
    inside = (row >= first) & (row < first + CLASS_BLOCK)
    swapped = lax.axis_index("dom") == 1
    allowed = [blocks_ref[0:1], blocks_ref[1:2]]
    precisions = [particle_row(p[...].astype(jnp.float32) * LOG2_E) for p in (prec_a, prec_b)]
    for half in range(2):
        lanes = slice(half * LANES, (half + 1) * LANES)
        admit = jnp.where(swapped, allowed[1 - half], allowed[half]) == 1
        admit = jnp.sum(jnp.where(inside & admit, 1.0, 0.0), axis=1, keepdims=True)
        base_ref[:, lanes] = jnp.where(admit > 0.0, -0.5 * norm_ref[...] * precisions[half], EXCLUDED)
        offset = particle_row((offset_a, offset_b)[half][...])
        steps = lax.rem(lax.broadcasted_iota(jnp.int32, (40, LANES), 0) - offset + ROTATIONS, ROTATIONS)
        distance = jnp.minimum(steps, ROTATIONS - steps).astype(jnp.float32) * (1.0 / PRIOR_WIDTH)
        prior_ref[:, lanes] = (-0.5 * LOG2_E) * distance * distance
    correlate(other_ref, cp_ref, xp_ref, ab_other)

    for half in range(2):
        lanes = slice(half * LANES, (half + 1) * LANES)
        prec = jnp.broadcast_to(precisions[half], (8, LANES))
        ab_ref = (ab_own, ab_other)[half]

        def scores(i, carry):
            peak, mass = carry
            rows = pl.ds(pl.multiple_of(i * 8, 8), 8)
            a = [ab_ref[j, rows] * prec for j in range(19)]
            b = [None] + [ab_ref[18 + j, rows] * prec for j in range(1, 18)]
            a[0] = a[0] + base_ref[rows, lanes]
            score = to_rotations(a, b)
            score = [score[r] + prior_ref[r : r + 1, lanes] for r in range(ROTATIONS)]
            top = score[0]
            for r in range(1, ROTATIONS):
                top = jnp.maximum(top, score[r])
            total = None
            for r in range(ROTATIONS):
                e = jnp.exp2(score[r] - top)
                e_ref[r, rows, lanes] = e
                total = e if total is None else total + e
            top_ref[rows, lanes] = top
            higher = jnp.maximum(peak, top)
            mass = mass * jnp.exp2(peak - higher) + total * jnp.exp2(top - higher)
            return higher, mass

        start = (jnp.full((8, LANES), EXCLUDED, jnp.float32), jnp.zeros((8, LANES), jnp.float32))
        tops, mass = lax.fori_loop(0, ROWS // 8, scores, start, unroll=True)
        peak = jnp.max(tops, axis=0, keepdims=True)
        mass = jnp.sum(mass * jnp.exp2(tops - peak), axis=0, keepdims=True)
        stat_ref[0:8, lanes] = jnp.broadcast_to(peak, (8, LANES))
        stat_ref[8:16, lanes] = jnp.broadcast_to(mass, (8, LANES))


def spectrum_kernel(e_ref, top_ref, stat_ref, w_ref):
    for half in range(2):
        lanes = slice(half * LANES, (half + 1) * LANES)

        peak = stat_ref[0:8, lanes]

        def spectra(i, carry):
            rows = pl.ds(pl.multiple_of(i * 8, 8), 8)
            lift = jnp.exp2(top_ref[rows, lanes] - peak)
            c, s = from_rotations([e_ref[r, rows, lanes] * lift for r in range(ROTATIONS)])
            for j in range(19):
                w_ref[j, rows, lanes] = c[j]
            for j in range(1, 18):
                w_ref[18 + j, rows, lanes] = s[j]
            return carry

        lax.fori_loop(0, ROWS // 8, spectra, 0, unroll=True)


def sign_kernel(sign_ref):
    for j in range(RESIDUES):
        sign_ref[j : j + 1] = sign_lanes(j, 1)


def own_kernel(cls_ref, sign_ref, own_ref, cp_ref, norm_ref, xp_ref, ab_ref):
    pad = jnp.zeros((ROWS_16 - CLASSES, LANES), jnp.bfloat16)
    for part in range(2):
        tiles = lambda t: cls_ref[:, part * PART + t * LANES : part * PART + (t + 1) * LANES]
        for j, value in to_residues(tiles, CLASSES):
            value = jnp.concatenate([value, pad], axis=0)
            cp_ref[j, :ROWS_16, part * LANES : (part + 1) * LANES] = value
            if 0 < j < 18:
                sign = jnp.broadcast_to(sign_ref[j : j + 1], (ROWS_16, LANES)) * (1.0 if part else -1.0)
                cp_ref[j, ROWS_16:, (1 - part) * LANES : (2 - part) * LANES] = value * sign.astype(jnp.bfloat16)
    norm = jnp.zeros((CLASSES, LANES), jnp.float32)
    for block in range(BLOCKS):
        member = cls_ref[:, block * LANES : (block + 1) * LANES].astype(jnp.float32)
        norm = norm + member * member
    norm = jnp.broadcast_to(jnp.sum(norm, axis=1, keepdims=True), (CLASSES, LANES))
    norm_ref[...] = jnp.concatenate([norm, jnp.zeros((ROWS - CLASSES, LANES), jnp.float32)], axis=0)
    correlate(own_ref, cp_ref, xp_ref, ab_ref)


def settle(mine, theirs, half):
    here = slice(half * LANES, (half + 1) * LANES)
    there = slice((1 - half) * LANES, (2 - half) * LANES)
    peak = jnp.maximum(mine[0:1, here], theirs[0:1, there])
    mass = mine[8:9, here] * jnp.exp2(mine[0:1, here] - peak)
    mass = mass + theirs[8:9, there] * jnp.exp2(theirs[0:1, there] - peak)
    held = lax.broadcasted_iota(jnp.int32, (1, LANES), 1) < OWN
    return held, peak, jnp.where(held, mass, 1.0)


def sums_kernel(w_ref, xp_own, xp_other, mine, theirs, out_ref, pc_ref):
    scale = []
    for half in range(2):
        held, peak, mass = settle(mine, theirs, half)
        lift = jnp.exp2(mine[0:1, half * LANES : (half + 1) * LANES] - peak)
        scale.append(jnp.where(held, lift * SUM_SCALE / mass, 0.0))
    scale = jnp.concatenate(scale, axis=1)

    def weights_of(i):
        return w_ref[i] * scale

    totals = weights_of(0)
    totals = jnp.concatenate([totals, jnp.zeros((LANES - ROWS, COLS), jnp.float32)], axis=0)
    high = totals.astype(jnp.bfloat16)
    low = (totals - high.astype(jnp.float32)).astype(jnp.bfloat16)
    ones = jnp.ones((16, COLS), jnp.bfloat16)
    dims = (((1,), (1,)), ((), ()))
    total = lax.dot_general(ones, high, dims, preferred_element_type=jnp.float32)
    total = total + lax.dot_general(ones, low, dims, preferred_element_type=jnp.float32)
    total = total[0:1]

    for j in range(RESIDUES):
        pair = 0 < j < 18
        weight = weights_of(j)
        if pair:
            weight = jnp.concatenate([weight, weights_of(18 + j)], axis=0)
        else:
            weight = jnp.concatenate([weight, jnp.zeros((8, COLS), jnp.float32)], axis=0)
        high = weight.astype(jnp.bfloat16)
        low = (weight - high.astype(jnp.float32)).astype(jnp.bfloat16)
        lanes = slice(j * COLS, (j + 1) * COLS)
        images = jnp.concatenate([xp_own[:, lanes], xp_other[:, lanes]], axis=0)
        dims = (((1,), (0,)), ((), ()))
        got = lax.dot_general(high, images, dims, preferred_element_type=jnp.float32)
        got = got + lax.dot_general(low, images, dims, preferred_element_type=jnp.float32)
        re, im = got[:ROWS, :LANES], got[:ROWS, LANES:]
        if pair:
            sign = sign_lanes(j, ROWS)
            re, im = re - sign * got[ROWS:, LANES:], im + sign * got[ROWS:, :LANES]
        pc_ref[:, j * COLS : j * COLS + LANES] = re
        pc_ref[:, j * COLS + LANES : (j + 1) * COLS] = im

    quarter = quarter_of(8)
    last = jnp.broadcast_to(total, (4, LANES))
    for part in range(2):
        for i in range(ROWS // 8):
            rotated = Rotated(lambda j: pc_ref[i * 8 : (i + 1) * 8, j * COLS + part * LANES : j * COLS + (part + 1) * LANES])
            for t in range(BLOCKS // 2):
                pieces = {m % GROUP: rotated(PLACE[m][0], m - PLACE[m][1]) for m in range(t * GROUP, (t + 1) * GROUP)}
                value = by_quarter(pieces, quarter)
                half, at = divmod(i, SPLIT // 8) if i < ROWS // 8 - 1 else (1, i - SPLIT // 8)
                block = half * BLOCKS + part * (BLOCKS // 2) + t
                if i == ROWS // 8 - 1:
                    out_ref[block, QUADS - 1] = value[:4]
                else:
                    out_ref[block, 2 * at : 2 * at + 2] = value.reshape(2, 4, LANES)
                if half == 0 and at == 0:
                    out_ref[block, QUADS - 1] = last


FINISH_STEPS = 4
STEP_BLOCKS = BLOCKS // FINISH_STEPS


def finish_kernel(sum_ref, cls_ref, mine, theirs, out_hbm, evidence_hbm, out_ref, evidence_ref, out_sems, evidence_sem):
    _, peak, mass = settle(mine, theirs, 0)
    evidence_ref[...] = (peak * (1.0 / LOG2_E) + jnp.log(mass))[:, :OWN]
    send = pltpu.make_async_copy(evidence_ref, evidence_hbm, evidence_sem)
    send.start()
    row = lax.broadcasted_iota(jnp.int32, (HALF_ROWS, LANES), 0)
    lane = lax.broadcasted_iota(jnp.int32, (HALF_ROWS, LANES), 1)
    share = []
    total = sum_ref[0, 0, SPLIT // 4, 0:1, :]
    for half in range(2):
        weight = jnp.sum(jnp.where(lane == row + half * SPLIT, total, 0.0), axis=1, keepdims=True)
        share.append((1.0 / SUM_SCALE) / (weight * (1.0 / SUM_SCALE) + CLASS_PRIOR))
    copies = []
    for step in range(FINISH_STEPS):
        for block in range(step * STEP_BLOCKS, (step + 1) * STEP_BLOCKS):
            lanes = slice(block * LANES, (block + 1) * LANES)
            old = cls_ref[:, lanes].astype(jnp.float32)
            for half in range(2):
                count = SPLIT if half == 0 else CLASSES - SPLIT
                rows = slice(half * SPLIT, half * SPLIT + count)
                new = sum_ref[half, block].reshape(HALF_ROWS, LANES)[:count] + (CLASS_PRIOR * SUM_SCALE) * old[rows]
                out_ref[rows, lanes] = new * share[half][:count]
        lanes = slice(step * STEP_BLOCKS * LANES, (step + 1) * STEP_BLOCKS * LANES)
        copy = pltpu.make_async_copy(out_ref.at[:, lanes], out_hbm.at[:, lanes], out_sems.at[step])
        copy.start()
        copies.append(copy)
    for copy in copies:
        copy.wait()
    send.wait()


VMEM = pl.BlockSpec(memory_space=pltpu.VMEM)


ANY = pl.BlockSpec(memory_space=pl.ANY)
MIB = 1024 * 1024


def shards(images, precision, rotation_offset, classes, prior_blocks):
    swap = [(0, 1), (1, 0)]
    other_images = lax.ppermute(images, "dom", swap)
    other_precision = lax.ppermute(precision, "dom", swap)
    other_offset = lax.ppermute(rotation_offset, "dom", swap)

    cost = pl.CostEstimate(flops=4 * 10**9, bytes_accessed=8 * MIB, transcendentals=36 * 104 * 128)
    signs = pl.pallas_call(
        sign_kernel,
        out_shape=jax.ShapeDtypeStruct((RESIDUES, LANES), jnp.float32),
        out_specs=VMEM,
        compiler_params=pltpu.CompilerParams(vmem_limit_bytes=4 * MIB),
        cost_estimate=cost,
        name="signs",
    )()
    cp, norm, xp_own, ab_own = pl.pallas_call(
        own_kernel,
        out_shape=(
            jax.ShapeDtypeStruct((RESIDUES, 2 * ROWS_16, COLS), jnp.bfloat16),
            jax.ShapeDtypeStruct((ROWS, LANES), jnp.float32),
            jax.ShapeDtypeStruct((LANES, RESIDUES * COLS), jnp.bfloat16),
            jax.ShapeDtypeStruct((36, ROWS, LANES), jnp.float32),
        ),
        in_specs=[VMEM] * 3,
        out_specs=(VMEM,) * 4,
        compiler_params=pltpu.CompilerParams(vmem_limit_bytes=16 * MIB),
        cost_estimate=cost,
        name="own",
    )(classes, signs, images)

    e, xp_other, mine, tops = pl.pallas_call(
        score_kernel,
        out_shape=(
            jax.ShapeDtypeStruct((36, ROWS, COLS), jnp.float32),
            jax.ShapeDtypeStruct((LANES, RESIDUES * COLS), jnp.bfloat16),
            jax.ShapeDtypeStruct((16, COLS), jnp.float32),
            jax.ShapeDtypeStruct((ROWS, COLS), jnp.float32),
        ),
        in_specs=[VMEM] * 9,
        out_specs=(VMEM,) * 4,
        scratch_shapes=[
            pltpu.VMEM((36, ROWS, LANES), jnp.float32),
            pltpu.VMEM((ROWS, COLS), jnp.float32),
            pltpu.VMEM((40, COLS), jnp.float32),
        ],
        compiler_params=pltpu.CompilerParams(vmem_limit_bytes=20 * MIB),
        cost_estimate=cost,
        name="scores",
    )(
        prior_blocks,
        other_images,
        precision.reshape(1, OWN),
        other_precision.reshape(1, OWN),
        rotation_offset.reshape(1, OWN),
        other_offset.reshape(1, OWN),
        cp,
        norm,
        ab_own,
    )
    theirs = lax.ppermute(mine, "dom", swap)

    weights = pl.pallas_call(
        spectrum_kernel,
        out_shape=jax.ShapeDtypeStruct((36, ROWS, COLS), jnp.float32),
        in_specs=[VMEM] * 3,
        out_specs=VMEM,
        compiler_params=pltpu.CompilerParams(vmem_limit_bytes=16 * MIB),
        cost_estimate=cost,
        name="spectra",
    )(e, tops, mine)

    parts = pl.pallas_call(
        sums_kernel,
        out_shape=jax.ShapeDtypeStruct((CHUNKS, QUADS, 4, LANES), jnp.float32),
        in_specs=[VMEM] * 5,
        out_specs=VMEM,
        scratch_shapes=[pltpu.VMEM((ROWS, RESIDUES * COLS), jnp.float32)],
        compiler_params=pltpu.CompilerParams(vmem_limit_bytes=20 * MIB),
        name="sums",
    )(weights, xp_own, xp_other, mine, theirs)

    flat = lax.optimization_barrier(parts.reshape(CHUNKS * HALF_ROWS, LANES))
    flat = lax.optimization_barrier(flat.astype(jnp.float16))
    got = lax.all_to_all(flat.reshape(parts.shape), "cls", 0, 0, tiled=True)
    pairs = lax.optimization_barrier(got.reshape(CHUNKS // 2, 2 * HALF_ROWS, LANES)).astype(jnp.float32).sum(axis=0)
    total = (pairs + jnp.roll(pairs, HALF_ROWS, axis=0)).astype(jnp.float16)
    repeated = lax.optimization_barrier(jnp.broadcast_to(total[None], (CHUNKS // 2, 2 * HALF_ROWS, LANES)))
    repeated = repeated.reshape(CHUNKS, QUADS, 4, LANES)
    whole = lax.all_to_all(repeated, "cls", 0, 0, tiled=True)
    new_classes, evidence = pl.pallas_call(
        finish_kernel,
        out_shape=(
            jax.ShapeDtypeStruct((CLASSES, BLOCKS * LANES), jnp.float32),
            jax.ShapeDtypeStruct((1, OWN), jnp.float32),
        ),
        in_specs=[VMEM] * 4,
        out_specs=(ANY, ANY),
        scratch_shapes=[
            pltpu.VMEM((CLASSES, BLOCKS * LANES), jnp.float32),
            pltpu.VMEM((1, OWN), jnp.float32),
            pltpu.SemaphoreType.DMA((FINISH_STEPS,)),
            pltpu.SemaphoreType.DMA,
        ],
        compiler_params=pltpu.CompilerParams(vmem_limit_bytes=12 * MIB),
        name="finish",
    )(lax.optimization_barrier(lax.optimization_barrier(whole.reshape(CHUNKS * HALF_ROWS, LANES)).astype(jnp.float32)).reshape(2, BLOCKS, QUADS, 4, LANES), classes, mine, theirs)
    return new_classes, evidence.reshape(OWN)


def solution(mesh):
    in_specs = (
        P(("cls", "dom"), None),
        P(("cls", "dom")),
        P(("cls", "dom")),
        P("dom", None),
        P("cls", "dom"),
    )
    out_specs = (P("dom", None), P(("cls", "dom")))
    return jax.shard_map(shards, mesh=mesh, in_specs=in_specs, out_specs=out_specs, check_vma=False)
```
